32 devices in a mesh: patch: 2 (over x), epoch: 16 (over z, y, core).
Axes of the slice: x: 2, y: 2, z: 4, core: 2. Of those that a mesh axis runs over, the one named last changes fastest.
Arguments:
- epoch_images: float32 [32, 64, 4096], P(('patch', 'epoch')), parts along dimension 0, may hold values from -8 to 8
- mask_words: int32 [32, 1, 128], P(('patch', 'epoch')), parts along dimension 0, may hold values from -2147483648 to 2147483647, as said below
- coefficients: float32 [32, 49, 3], P('patch'), parts along dimension 0, may hold values from -2 to 2
- epoch_order: int32 [32], P('patch'), parts along dimension 0, may hold values from 0 to 15, each once
Outputs:
- difference: float32 [32, 32, 4096], P(('patch', 'epoch')), parts along dimension 0
The draws below stay inside these ranges and needn't reach their ends.
There are 2 independent parts, one for each index of `patch`. The reference program is written for one: setup_inputs(seed, part) draws one part's arguments, and reference() takes and returns one part's arrays. A program takes and returns all parts, laid end to end along the dimension named above; each array names one. Nothing has to cross between parts.
Inputs may be any that keep to these rules, and one draw needn't show every extreme that they name: `mask_words`: bit b of word w in band n of an epoch marks column 32 w + b of rows n * 64 to (n + 1) * 64 - 1 of that epoch valid (1) or masked (0), bit 31 being the sign bit; some cells are masked in every epoch. A permutation: image slot e uses the coefficients of catalog epoch epoch_order[e].
All inputs are finite; a program needn't handle non-finite values.
Results may differ from the reference program's by a relative error of at most 0.000057.
Values sent between devices are 32-bit elements; how exact they have to be, the bound alone decides.
A program may use at most 64 MiB of HBM per device.

```python
import math
import jax
import jax.numpy as jnp
from jax import lax

W = 4096
ROWS = 32
HALF = 15
MARGIN = 16
BAND = 64
KERNELS = 49
POLY = 3
EPOCHS = 16


def draw_epoch_images(key, part):
    sky_key = jax.random.fold_in(key, 101)
    noise_key = jax.random.fold_in(key, 202)
    padded_rows = ROWS + 2 * MARGIN
    sky_field = jax.random.normal(sky_key, (padded_rows, W), jnp.float32)
    noise_field = jax.random.normal(noise_key, (EPOCHS, padded_rows, W), jnp.float32)
    return jnp.clip(sky_field[None] + noise_field, -8.0, 8.0)


def draw_mask_words(key, part):
    bands = (ROWS + 2 * MARGIN) // BAND
    common = jax.random.randint(jax.random.fold_in(key, 11), (bands, W), 0, 64) == 0
    epoch_good = jax.random.randint(jax.random.fold_in(key, 12), (EPOCHS, bands, W), 0, 8) != 0
    good_bits = jnp.logical_and(epoch_good, jnp.logical_not(common[None])).astype(jnp.int32)
    good_bits = good_bits.reshape(EPOCHS, bands, W // 32, 32)
    placed = jnp.left_shift(good_bits, jnp.arange(32, dtype=jnp.int32))
    return jnp.sum(placed, axis=-1, dtype=jnp.int32)


def scatter_about(rng, dims, deviation, limit, held_as=jnp.bfloat16):
    drawn = jax.random.normal(rng, dims, jnp.float32) * deviation
    return jnp.minimum(jnp.maximum(drawn, -limit), limit).astype(held_as)


def setup_inputs(seed: int = 0, part: int = 0) -> dict:
    arg_keys = jax.random.split(jax.random.key(seed), 5)
    part_keys = jax.random.split(jax.random.fold_in(arg_keys[4], part), 5)
    epoch_images = draw_epoch_images(jax.random.fold_in(jax.random.fold_in(arg_keys[4], part), 71), part)
    mask_words = draw_mask_words(jax.random.fold_in(jax.random.fold_in(arg_keys[4], part), 71), part)
    coefficients = scatter_about(part_keys[2], (EPOCHS, KERNELS, POLY), 0.3, 2.0, jnp.float32)
    epoch_order = jax.random.permutation(part_keys[3], EPOCHS).astype(jnp.int32)
    return dict(epoch_images=epoch_images, mask_words=mask_words, coefficients=coefficients, epoch_order=epoch_order)


gauss_widths = (1.5, 3.0, 6.0)
gauss_degrees = (6, 4, 2)

def basis_filters(half_width):
    offsets = jnp.arange(-half_width, half_width + 1).astype(jnp.float32)
    result = []
    for spread_width, degree in zip(gauss_widths, gauss_degrees):
        envelope = jnp.exp(-offsets * offsets / (2.0 * spread_width * spread_width)) / (math.sqrt(2.0 * math.pi) * spread_width)
        for vert_power in range(degree + 1):
            result.append(envelope * (offsets / spread_width) ** vert_power)
    return jnp.stack(result)

def kernel_pairs():
    result = []
    first_index = 0
    for degree in gauss_degrees:
        for vert_power in range(degree + 1):
            for horiz_power in range(degree + 1 - vert_power):
                result.append((first_index + vert_power, first_index + horiz_power))
        first_index = first_index + degree + 1
    return result

def unpack_valid(mask_words):
    bit_places = jnp.arange(32, dtype=jnp.int32)
    bit_values = jnp.right_shift(mask_words[..., None], bit_places) & 1
    word_shape = mask_words.shape
    return bit_values.reshape(word_shape[0], word_shape[1], word_shape[2] * 32).astype(jnp.float32)

def reference(epoch_images, mask_words, coefficients, epoch_order):
    band_valid = unpack_valid(mask_words)
    valid_mask = jnp.repeat(band_valid, BAND, axis=1)
    masked_sum = lax.optimization_barrier(jnp.sum(valid_mask * epoch_images, axis=0))
    counts = jnp.repeat(lax.optimization_barrier(jnp.sum(band_valid, axis=0)), BAND, axis=0)
    template = masked_sum / jnp.maximum(counts, 1.0)
    filters = basis_filters(HALF)
    tap_count = 2 * HALF + 1
    vertical = []
    for filter_index in range(filters.shape[0]):
        running = jnp.zeros((ROWS, W), jnp.float32)
        for offset in range(tap_count):
            start_row = MARGIN - HALF + offset
            running = running + filters[filter_index, offset] * template[start_row:start_row + ROWS]
        vertical.append(running)
    vertical = jnp.stack(vertical)
    padded = jnp.pad(vertical, ((0, 0), (0, 0), (HALF, HALF)))
    convolved = []
    for vert_index, horiz_index in kernel_pairs():
        running = jnp.zeros((ROWS, W), jnp.float32)
        for offset in range(tap_count):
            running = running + filters[horiz_index, offset] * padded[vert_index, :, offset:offset + W]
        convolved.append(running)
    convolved = jnp.stack(convolved)
    columns = (2.0 * jnp.arange(W).astype(jnp.float32) + 1.0) / W - 1.0
    row_pos = (2.0 * jnp.arange(ROWS).astype(jnp.float32) + 1.0) / ROWS - 1.0
    spatial = jnp.stack([jnp.ones((ROWS, W), jnp.float32), jnp.broadcast_to(columns[None, :], (ROWS, W)), jnp.broadcast_to(row_pos[:, None], (ROWS, W))])
    basis_images = (convolved[:, None] * spatial[None]).reshape(KERNELS * POLY, ROWS * W)
    coef_table = coefficients[epoch_order].reshape(EPOCHS, KERNELS * POLY)
    model_image = jnp.dot(coef_table, basis_images, precision=lax.Precision.HIGHEST, preferred_element_type=jnp.float32).reshape(EPOCHS, ROWS, W)
    centre = epoch_images[:, MARGIN:MARGIN + ROWS]
    return valid_mask[:, MARGIN:MARGIN + ROWS] * (centre - model_image)
```

```python
import math

import jax
import jax.numpy as jnp
import ml_dtypes
import numpy as np
from jax import lax
from jax.experimental import pallas as pl
from jax.experimental.pallas import tpu as pltpu
from jax.sharding import PartitionSpec as P

HALF = 15
MARGIN = 16
BAND = 64
KERNELS = 49
POLY = 3
LANES = 128


gauss_widths = (1.5, 3.0, 6.0)
gauss_degrees = (6, 4, 2)


def extended(cells, sides, width):
    for axis, dim in sides:
        count = lax.axis_size(axis)
        ends = count - 1
        head = lax.slice_in_dim(cells, 0, width, axis=dim)
        tail = lax.slice_in_dim(cells, cells.shape[dim] - width, cells.shape[dim], axis=dim)
        cells = jnp.concatenate(
            [
                lax.ppermute(tail, axis, [(i, (i + 1) % count) for i in range(ends)]),
                cells,
                lax.ppermute(head, axis, [((i + 1) % count, i) for i in range(ends)]),
            ],
            axis=dim,
        )
    return cells


def basis_filters(half_width):
    offsets = jnp.arange(-half_width, half_width + 1).astype(jnp.float32)
    result = []
    for spread_width, degree in zip(gauss_widths, gauss_degrees):
        envelope = jnp.exp(-offsets * offsets / (2.0 * spread_width * spread_width)) / (
            math.sqrt(2.0 * math.pi) * spread_width
        )
        for vert_power in range(degree + 1):
            result.append(envelope * (offsets / spread_width) ** vert_power)
    return jnp.stack(result)


def kernel_pairs():
    result = []
    first_index = 0
    for degree in gauss_degrees:
        for vert_power in range(degree + 1):
            for horiz_power in range(degree + 1 - vert_power):
                result.append((first_index + vert_power, first_index + horiz_power))
        first_index = first_index + degree + 1
    return result


def unpack_valid(mask_words):
    bit_places = jnp.arange(32, dtype=jnp.int32)
    bit_values = jnp.right_shift(mask_words[..., None], bit_places) & 1
    word_shape = mask_words.shape
    return bit_values.reshape(word_shape[0], word_shape[1], word_shape[2] * 32).astype(jnp.float32)


def shift_table(tap_count, inner_cols, outer_cols):
    taps_axis = jnp.arange(tap_count)[:, None, None]
    inner_axis = jnp.arange(inner_cols)[None, :, None]
    outer_axis = jnp.arange(outer_cols)[None, None, :]
    return (inner_axis - outer_axis == taps_axis).astype(jnp.float32)


def vertical_matrices(filters, rows_out, padded_rows):
    tap_count = filters.shape[1]
    out_rows = jnp.arange(rows_out)[:, None]
    in_rows = jnp.arange(padded_rows)[None, :]
    places = in_rows - out_rows - MARGIN + HALF
    one_hot = (places[None] == jnp.arange(tap_count)[:, None, None]).astype(jnp.float32)
    return jnp.einsum("jd,drt->jrt", filters, one_hot, precision=lax.Precision.HIGHEST)


def spatial_terms(col_start, col_count, total_columns, rows_out):
    columns = (
        2.0 * (col_start + jnp.arange(col_count)).astype(jnp.float32) + 1.0
    ) / total_columns - 1.0
    row_pos = (2.0 * jnp.arange(rows_out).astype(jnp.float32) + 1.0) / rows_out - 1.0
    return jnp.stack(
        [
            jnp.ones((rows_out, col_count), jnp.float32),
            jnp.broadcast_to(columns[None, :], (rows_out, col_count)),
            jnp.broadcast_to(row_pos[:, None], (rows_out, col_count)),
        ]
    )


def shards(epoch_images, mask_words, coefficients, epoch_order):
    slot_count, padded_rows, total_columns = epoch_images.shape
    rows_out = padded_rows - 2 * MARGIN
    band_valid = unpack_valid(mask_words)
    valid_mask = jnp.repeat(band_valid, BAND, axis=1)
    part_total = jnp.sum(valid_mask * epoch_images, axis=0)
    part_count = jnp.sum(band_valid, axis=0)
    filters = basis_filters(HALF)
    pair_list = kernel_pairs()
    vert_table = np.zeros((len(pair_list), filters.shape[0]), np.float32)
    horiz_table = np.zeros((len(pair_list), filters.shape[0]), np.float32)
    for kernel_index, pair_value in enumerate(pair_list):
        vert_table[kernel_index, pair_value[0]] = 1.0
        horiz_table[kernel_index, pair_value[1]] = 1.0
    vert_pick = jnp.asarray(vert_table)
    horiz_filters = jnp.dot(jnp.asarray(horiz_table), filters, precision=lax.Precision.HIGHEST)
    vert_mats = vertical_matrices(filters, rows_out, padded_rows)
    full_sum, full_count = (
        lax.psum_scatter(part_total, "epoch", scatter_dimension=1, tiled=True),
        lax.psum_scatter(part_count, "epoch", scatter_dimension=1, tiled=True),
    )
    template = full_sum / jnp.maximum(jnp.repeat(full_count, BAND, axis=0), 1.0)
    slab_cols = template.shape[1]
    rimmed = extended(template, (("epoch", 1),), HALF)
    vertical = jnp.einsum("jrt,tc->jrc", vert_mats, rimmed, precision=lax.Precision.HIGHEST)
    picked = jnp.einsum("kj,jrc->krc", vert_pick, vertical, precision=lax.Precision.HIGHEST)
    horiz_mats = jnp.einsum(
        "kd,dso->kso",
        horiz_filters,
        shift_table(horiz_filters.shape[1], slab_cols + 2 * HALF, slab_cols),
        precision=lax.Precision.HIGHEST,
    )
    convolved = jnp.einsum("krs,kso->kro", picked, horiz_mats, precision=lax.Precision.HIGHEST)
    spatial = spatial_terms(lax.axis_index("epoch") * slab_cols, slab_cols, total_columns, rows_out)
    term_count = coefficients.shape[1] * coefficients.shape[2]
    basis_images = (convolved[:, None] * spatial[None]).reshape(term_count, rows_out * slab_cols)
    coef_table = coefficients[epoch_order].reshape(coefficients.shape[0], term_count)
    models = jnp.dot(
        coef_table,
        basis_images,
        precision=lax.Precision.HIGHEST,
        preferred_element_type=jnp.float32,
    ).reshape(coefficients.shape[0], rows_out, slab_cols)
    model_image = lax.all_to_all(models, "epoch", split_axis=0, concat_axis=2, tiled=True)
    centre = epoch_images[:, MARGIN : MARGIN + rows_out]
    return valid_mask[:, MARGIN : MARGIN + rows_out] * (centre - model_image)


def filter_values():
    offsets = np.arange(-HALF, HALF + 1).astype(np.float64)
    groups = []
    for spread, degree in zip(gauss_widths, gauss_degrees):
        envelope = np.exp(-offsets * offsets / (2.0 * spread * spread)) / (math.sqrt(2.0 * math.pi) * spread)
        groups.append([envelope * (offsets / spread) ** power for power in range(degree + 1)])
    return groups


def split_constant(values):
    values = values.astype(np.float32)
    high = values.astype(ml_dtypes.bfloat16)
    low = (values - high.astype(np.float32)).astype(ml_dtypes.bfloat16)
    return high, low


def kernel_constants(rows_out, padded_rows):
    groups = filter_values()
    vert = np.zeros((len(groups), rows_out, 8, padded_rows))
    for g, filters in enumerate(groups):
        for j, taps in enumerate(filters):
            for r in range(rows_out):
                start = r + MARGIN - HALF
                vert[g, r, j, start : start + taps.shape[0]] = taps
    vert = vert.reshape(len(groups) * rows_out * 8, padded_rows)
    high, low = split_constant(vert)
    vert_stack = np.concatenate([high, high, low], axis=1)
    flat = [taps for filters in groups for taps in filters]
    horiz = np.zeros((2 * LANES, len(flat), LANES))
    for h, taps in enumerate(flat):
        for o in range(LANES):
            start = o + LANES // 2 - HALF
            horiz[start : start + taps.shape[0], h, o] = taps
    horiz_stack = np.stack(split_constant(horiz.reshape(2 * LANES, len(flat) * LANES)))
    place = np.zeros((KERNELS, LANES), np.float32)
    index, base = 0, 0
    for degree in gauss_degrees:
        for a in range(degree + 1):
            for b in range(degree + 1 - a):
                place[index, (base + b) * 8 + a] = 1.0
                index += 1
        base += degree + 1
    return vert_stack, horiz_stack, place


def split(values):
    high = values.astype(jnp.bfloat16)
    return high, (values - high.astype(jnp.float32)).astype(jnp.bfloat16)


def dot32(a, b):
    return jnp.dot(a, b, preferred_element_type=jnp.float32)


def exact(a, b):
    return jnp.dot(a, b, precision=lax.Precision.HIGHEST, preferred_element_type=jnp.float32)


def strip_kernel(
    image, words, coef, order, place, vert_hbm, horiz_hbm, out,
    sums, got_core, got_y, got_z, ext, valid, vert, horiz, v_high, v_low, conv, mix, models, got,
    const_sem, send_core, recv_core, send_y, recv_y, send_z, recv_z, send_halo, recv_halo, send_model, recv_model,
):
    count = 16
    zs = count // 4
    slab = 2 * LANES
    me = lax.axis_index("epoch")
    k = lax.rem(me, 2)
    y = lax.rem(me // 2, 2)
    z = me // 4

    def remote(src, dst, ssem, rsem, device):
        return pltpu.make_async_remote_copy(
            src_ref=src, dst_ref=dst, send_sem=ssem, recv_sem=rsem,
            device_id={"epoch": device}, device_id_type=pl.DeviceIdType.MESH,
        )

    barrier = pltpu.get_barrier_semaphore()
    for d in range(1, count):
        pl.semaphore_signal(
            barrier, inc=1, device_id={"epoch": lax.rem(me + d, count)}, device_id_type=pl.DeviceIdType.MESH
        )
    copy_vert = pltpu.make_async_copy(vert_hbm, vert, const_sem.at[0])
    copy_horiz = pltpu.make_async_copy(horiz_hbm, horiz, const_sem.at[1])
    copy_vert.start()
    copy_horiz.start()

    lane = lax.broadcasted_iota(jnp.int32, (8, LANES), 1)
    place_bit = lane & 31
    for q in range(count):
        for half in range(2):
            t = q * 2 + half
            word = jnp.where(
                lane < 64,
                jnp.where(lane < 32, words[4 * t], words[4 * t + 1]),
                jnp.where(lane < 96, words[4 * t + 2], words[4 * t + 3]),
            )
            bits = (jnp.right_shift(word, place_bit) & 1).astype(jnp.float32)
            valid[:, t * LANES : (t + 1) * LANES] = bits
            spot = sums.at[q % 2, (q // 2) % 2, q // 4]
            for s in range(0, 64, 8):
                spot[s : s + 8, half * LANES : (half + 1) * LANES] = (
                    bits * image[0, s : s + 8, t * LANES : (t + 1) * LANES]
                )
            spot[0:1, half * LANES : (half + 1) * LANES] = bits[0:1]
    pl.semaphore_wait(barrier, count - 1)

    core_copies = []
    for h, yy in enumerate((1 - y, y)):
        copy = remote(
            sums.at[1 - k, yy], got_core.at[yy], send_core.at[h], recv_core.at[h], me + 1 - 2 * k
        )
        copy.start()
        core_copies.append(copy)
    core_copies[0].wait_recv()
    ring = [lax.rem(z + d, zs) for d in (2, 1, 3, 0)]
    y_copies = []
    for zz in ring:
        sums[k, 1 - y, zz] = sums[k, 1 - y, zz] + got_core[1 - y, zz]
        copy = remote(sums.at[k, 1 - y, zz], got_y.at[zz], send_y.at[zz], recv_y.at[zz], me + 2 - 4 * y)
        copy.start()
        y_copies.append(copy)
    core_copies[1].wait_recv()
    for zz in ring:
        sums[k, y, zz] = sums[k, y, zz] + got_core[y, zz]

    slots = lax.broadcasted_iota(jnp.int32, (count, count), 1)
    pick = (slots == order[...]).astype(jnp.float32)
    for p in range(POLY):
        table = exact(exact(pick, coef[p]), place[...])
        high, low = split(table)
        rows = slice(p * count, (p + 1) * count)
        mix[rows, :LANES] = high
        mix[rows, LANES:] = high
        rows = slice((POLY + p) * count, (POLY + p + 1) * count)
        mix[rows, :LANES] = low
        mix[rows, LANES:] = jnp.zeros_like(low)

    z_copies = []
    for zz, copy in zip(ring, y_copies):
        copy.wait_recv()
        sums[k, y, zz] = sums[k, y, zz] + got_y[zz]
        if len(z_copies) < zs - 1:
            sent = remote(
                sums.at[k, y, zz], got_z.at[z], send_z.at[zz], recv_z.at[z], zz * 4 + lax.rem(me, 4)
            )
            sent.start()
            z_copies.append(sent)
    copy_vert.wait()
    copy_horiz.wait()
    for zz in ring[:-1]:
        remote(sums.at[k, y, zz], got_z.at[zz], send_z.at[zz], recv_z.at[zz], me).wait_recv()
    total = sums[k, y, z]
    for zz in ring[:-1]:
        total = total + got_z[zz]
    ext[:, LANES : 3 * LANES] = total / jnp.maximum(total[0:1], 1.0)

    left = lax.rem(me + count - 1, count)
    right = lax.rem(me + 1, count)
    halo = [
        remote(ext.at[:, LANES : 2 * LANES], ext.at[:, 3 * LANES :], send_halo.at[0], recv_halo.at[0], left),
        remote(ext.at[:, 2 * LANES : 3 * LANES], ext.at[:, :LANES], send_halo.at[1], recv_halo.at[1], right),
    ]
    for copy in halo:
        copy.start()
    for copy in halo:
        copy.wait_recv()
    first = jnp.where(me > 0, ext[:, :LANES], 0.0)
    last = jnp.where(me < count - 1, ext[:, 3 * LANES :], 0.0)
    joined = jnp.concatenate([first, ext[:, LANES : 3 * LANES], last], axis=1)
    half = LANES // 2
    windows = jnp.concatenate([joined[:, half : half + slab], joined[:, LANES + half : LANES + half + slab]], axis=1)
    high, low = split(windows)
    stacked = jnp.concatenate([high, low, high], axis=0)
    groups = len(gauss_degrees)
    block = 256
    for g in range(groups):
        rows = slice(g * block, (g + 1) * block)
        made = dot32(vert[rows, :], stacked)
        high, low = split(made)
        v_high[rows, :] = high
        v_low[rows, :] = low
    for w in range(2):
        base = 0
        for g, degree in enumerate(gauss_degrees):
            rows = slice(g * block, (g + 1) * block)
            cols = slice(w * slab, (w + 1) * slab)
            outs = slice(base * LANES, (base + degree + 1) * LANES)
            conv[w, :, outs] = (
                dot32(v_high[rows, cols], horiz[0, :, outs])
                + dot32(v_low[rows, cols], horiz[0, :, outs])
                + dot32(v_high[rows, cols], horiz[1, :, outs])
            )
            base += degree + 1

    column = me * slab + lax.broadcasted_iota(jnp.int32, (count, slab), 1)
    across = (2.0 * column.astype(jnp.float32) + 1.0) / (count * slab) - 1.0
    pairs = 15
    rows_out = 32

    def model_rows(blk, carry):
        for i in range(8):
            r = blk * 8 + i
            start = pl.multiple_of(r * 8, 8)
            sides = []
            for w in range(2):
                line = conv[w, pl.ds(start, 8), :]
                pieces = [line[:, h * LANES : (h + 1) * LANES] for h in range(pairs)]
                pieces.append(jnp.zeros((8, LANES), jnp.float32))
                sides.append(jnp.concatenate(pieces, axis=0))
            high, low = split(jnp.concatenate(sides, axis=1))
            made = dot32(mix[...], jnp.concatenate([high, low], axis=0))
            made = made[: POLY * count] + made[POLY * count :]
            down = (2.0 * lax.convert_element_type(r, jnp.float32) + 1.0) / rows_out - 1.0
            models[:, r, :] = made[:count] + across * made[count : 2 * count] + down * made[2 * count :]
        start = pl.multiple_of(blk * 8, 8)
        for d in ORDER:
            peer = lax.rem(me + d, count)
            remote(
                models.at[peer, pl.ds(start, 8)], got.at[me, pl.ds(start, 8)],
                send_model.at[blk, peer], recv_model.at[blk, me], peer,
            ).start()
        return carry

    lax.fori_loop(0, rows_out // 8, model_rows, 0)

    def finish(q, source):
        start = pl.multiple_of(q * slab, slab)
        seen = valid[:, pl.ds(start, slab)]
        for s in range(0, rows_out, 8):
            out[0, s : s + 8, pl.ds(start, slab)] = seen * (
                image[0, MARGIN + s : MARGIN + s + 8, pl.ds(start, slab)] - source[q, s : s + 8, :]
            )

    finish(me, models)
    for d in ORDER:
        q = lax.rem(me + count - d, count)
        for blk in range(rows_out // 8):
            rows = pl.ds(blk * 8, 8)
            remote(
                models.at[q, rows], got.at[q, rows], send_model.at[blk, q], recv_model.at[blk, q], q
            ).wait_recv()
        finish(q, got)

    for copy in core_copies + y_copies + z_copies + halo:
        copy.wait_send()
    for d in ORDER:
        peer = lax.rem(me + d, count)
        for blk in range(rows_out // 8):
            rows = pl.ds(blk * 8, 8)
            remote(
                models.at[peer, rows], got.at[me, rows], send_model.at[blk, peer], recv_model.at[blk, me], peer
            ).wait_send()


ORDER = (8, 7, 9, 6, 10, 5, 11, 4, 12, 3, 13, 2, 14, 1, 15)


def strip(epoch_images, mask_words, coefficients, epoch_order):
    vert, horiz, place = kernel_constants(32, 64)
    vmem = pl.BlockSpec(memory_space=pltpu.VMEM)
    smem = pl.BlockSpec(memory_space=pltpu.SMEM)
    anywhere = pl.BlockSpec(memory_space=pl.ANY)
    f32 = jnp.float32
    bf16 = jnp.bfloat16
    dma = pltpu.SemaphoreType.DMA
    return pl.pallas_call(
        strip_kernel,
        out_shape=jax.ShapeDtypeStruct((1, 32, 4096), f32),
        in_specs=[vmem, smem, vmem, vmem, vmem, anywhere, anywhere],
        out_specs=vmem,
        scratch_shapes=[
            pltpu.VMEM((2, 2, 4, 64, 256), f32),
            pltpu.VMEM((2, 4, 64, 256), f32),
            pltpu.VMEM((4, 64, 256), f32),
            pltpu.VMEM((4, 64, 256), f32),
            pltpu.VMEM((64, 512), f32),
            pltpu.VMEM((8, 4096), f32),
            pltpu.VMEM(vert.shape, bf16),
            pltpu.VMEM(horiz.shape, bf16),
            pltpu.VMEM((768, 512), bf16),
            pltpu.VMEM((768, 512), bf16),
            pltpu.VMEM((2, 256, 15 * LANES), f32),
            pltpu.VMEM((96, 256), bf16),
            pltpu.VMEM((16, 32, 256), f32),
            pltpu.VMEM((16, 32, 256), f32),
            dma((2,)),
            dma((2,)),
            dma((2,)),
            dma((4,)),
            dma((4,)),
            dma((4,)),
            dma((4,)),
            dma((2,)),
            dma((2,)),
            dma((4, 16)),
            dma((4, 16)),
        ],
        compiler_params=pltpu.CompilerParams(
            collective_id=0, has_side_effects=True, vmem_limit_bytes=40 * 1024 * 1024
        ),
        cost_estimate=pl.CostEstimate(flops=2 * 10**9, bytes_accessed=4 * 10**6, transcendentals=0),
    )(
        epoch_images,
        mask_words.reshape(-1),
        jnp.transpose(coefficients, (2, 0, 1)),
        epoch_order.reshape(-1, 1),
        jnp.asarray(place),
        jnp.asarray(vert),
        jnp.asarray(horiz),
    )


def solution(mesh):
    placed = (
        P(("patch", "epoch"), None, None),
        P(("patch", "epoch"), None, None),
        P("patch", None, None),
        P("patch"),
    )
    body = strip if mesh.shape["epoch"] == 16 else shards
    return jax.shard_map(
        body,
        mesh=mesh,
        in_specs=placed,
        out_specs=P(("patch", "epoch"), None, None),
        check_vma=False,
    )
```

```python
import math

import jax
import jax.numpy as jnp
import ml_dtypes
import numpy as np
from jax import lax
from jax.experimental import pallas as pl
from jax.experimental.pallas import tpu as pltpu
from jax.sharding import PartitionSpec as P

HALF = 15
MARGIN = 16
BAND = 64
KERNELS = 49
POLY = 3
LANES = 128


gauss_widths = (1.5, 3.0, 6.0)
gauss_degrees = (6, 4, 2)


def extended(cells, sides, width):
    for axis, dim in sides:
        count = lax.axis_size(axis)
        ends = count - 1
        head = lax.slice_in_dim(cells, 0, width, axis=dim)
        tail = lax.slice_in_dim(cells, cells.shape[dim] - width, cells.shape[dim], axis=dim)
        cells = jnp.concatenate(
            [
                lax.ppermute(tail, axis, [(i, (i + 1) % count) for i in range(ends)]),
                cells,
                lax.ppermute(head, axis, [((i + 1) % count, i) for i in range(ends)]),
            ],
            axis=dim,
        )
    return cells


def basis_filters(half_width):
    offsets = jnp.arange(-half_width, half_width + 1).astype(jnp.float32)
    result = []
    for spread_width, degree in zip(gauss_widths, gauss_degrees):
        envelope = jnp.exp(-offsets * offsets / (2.0 * spread_width * spread_width)) / (
            math.sqrt(2.0 * math.pi) * spread_width
        )
        for vert_power in range(degree + 1):
            result.append(envelope * (offsets / spread_width) ** vert_power)
    return jnp.stack(result)


def kernel_pairs():
    result = []
    first_index = 0
    for degree in gauss_degrees:
        for vert_power in range(degree + 1):
            for horiz_power in range(degree + 1 - vert_power):
                result.append((first_index + vert_power, first_index + horiz_power))
        first_index = first_index + degree + 1
    return result


def unpack_valid(mask_words):
    bit_places = jnp.arange(32, dtype=jnp.int32)
    bit_values = jnp.right_shift(mask_words[..., None], bit_places) & 1
    word_shape = mask_words.shape
    return bit_values.reshape(word_shape[0], word_shape[1], word_shape[2] * 32).astype(jnp.float32)


def shift_table(tap_count, inner_cols, outer_cols):
    taps_axis = jnp.arange(tap_count)[:, None, None]
    inner_axis = jnp.arange(inner_cols)[None, :, None]
    outer_axis = jnp.arange(outer_cols)[None, None, :]
    return (inner_axis - outer_axis == taps_axis).astype(jnp.float32)


def vertical_matrices(filters, rows_out, padded_rows):
    tap_count = filters.shape[1]
    out_rows = jnp.arange(rows_out)[:, None]
    in_rows = jnp.arange(padded_rows)[None, :]
    places = in_rows - out_rows - MARGIN + HALF
    one_hot = (places[None] == jnp.arange(tap_count)[:, None, None]).astype(jnp.float32)
    return jnp.einsum("jd,drt->jrt", filters, one_hot, precision=lax.Precision.HIGHEST)


def spatial_terms(col_start, col_count, total_columns, rows_out):
    columns = (
        2.0 * (col_start + jnp.arange(col_count)).astype(jnp.float32) + 1.0
    ) / total_columns - 1.0
    row_pos = (2.0 * jnp.arange(rows_out).astype(jnp.float32) + 1.0) / rows_out - 1.0
    return jnp.stack(
        [
            jnp.ones((rows_out, col_count), jnp.float32),
            jnp.broadcast_to(columns[None, :], (rows_out, col_count)),
            jnp.broadcast_to(row_pos[:, None], (rows_out, col_count)),
        ]
    )


def shards(epoch_images, mask_words, coefficients, epoch_order):
    slot_count, padded_rows, total_columns = epoch_images.shape
    rows_out = padded_rows - 2 * MARGIN
    band_valid = unpack_valid(mask_words)
    valid_mask = jnp.repeat(band_valid, BAND, axis=1)
    part_total = jnp.sum(valid_mask * epoch_images, axis=0)
    part_count = jnp.sum(band_valid, axis=0)
    filters = basis_filters(HALF)
    pair_list = kernel_pairs()
    vert_table = np.zeros((len(pair_list), filters.shape[0]), np.float32)
    horiz_table = np.zeros((len(pair_list), filters.shape[0]), np.float32)
    for kernel_index, pair_value in enumerate(pair_list):
        vert_table[kernel_index, pair_value[0]] = 1.0
        horiz_table[kernel_index, pair_value[1]] = 1.0
    vert_pick = jnp.asarray(vert_table)
    horiz_filters = jnp.dot(jnp.asarray(horiz_table), filters, precision=lax.Precision.HIGHEST)
    vert_mats = vertical_matrices(filters, rows_out, padded_rows)
    full_sum, full_count = (
        lax.psum_scatter(part_total, "epoch", scatter_dimension=1, tiled=True),
        lax.psum_scatter(part_count, "epoch", scatter_dimension=1, tiled=True),
    )
    template = full_sum / jnp.maximum(jnp.repeat(full_count, BAND, axis=0), 1.0)
    slab_cols = template.shape[1]
    rimmed = extended(template, (("epoch", 1),), HALF)
    vertical = jnp.einsum("jrt,tc->jrc", vert_mats, rimmed, precision=lax.Precision.HIGHEST)
    picked = jnp.einsum("kj,jrc->krc", vert_pick, vertical, precision=lax.Precision.HIGHEST)
    horiz_mats = jnp.einsum(
        "kd,dso->kso",
        horiz_filters,
        shift_table(horiz_filters.shape[1], slab_cols + 2 * HALF, slab_cols),
        precision=lax.Precision.HIGHEST,
    )
    convolved = jnp.einsum("krs,kso->kro", picked, horiz_mats, precision=lax.Precision.HIGHEST)
    spatial = spatial_terms(lax.axis_index("epoch") * slab_cols, slab_cols, total_columns, rows_out)
    term_count = coefficients.shape[1] * coefficients.shape[2]
    basis_images = (convolved[:, None] * spatial[None]).reshape(term_count, rows_out * slab_cols)
    coef_table = coefficients[epoch_order].reshape(coefficients.shape[0], term_count)
    models = jnp.dot(
        coef_table,
        basis_images,
        precision=lax.Precision.HIGHEST,
        preferred_element_type=jnp.float32,
    ).reshape(coefficients.shape[0], rows_out, slab_cols)
    model_image = lax.all_to_all(models, "epoch", split_axis=0, concat_axis=2, tiled=True)
    centre = epoch_images[:, MARGIN : MARGIN + rows_out]
    return valid_mask[:, MARGIN : MARGIN + rows_out] * (centre - model_image)


def filter_values():
    offsets = np.arange(-HALF, HALF + 1).astype(np.float64)
    groups = []
    for spread, degree in zip(gauss_widths, gauss_degrees):
        envelope = np.exp(-offsets * offsets / (2.0 * spread * spread)) / (math.sqrt(2.0 * math.pi) * spread)
        groups.append([envelope * (offsets / spread) ** power for power in range(degree + 1)])
    return groups


def split_constant(values):
    values = values.astype(np.float32)
    high = values.astype(ml_dtypes.bfloat16)
    low = (values - high.astype(np.float32)).astype(ml_dtypes.bfloat16)
    return high, low


def kernel_constants(rows_out, padded_rows):
    groups = filter_values()
    vert = np.zeros((len(groups), rows_out, 8, padded_rows))
    for g, filters in enumerate(groups):
        for j, taps in enumerate(filters):
            for r in range(rows_out):
                start = r + MARGIN - HALF
                vert[g, r, j, start : start + taps.shape[0]] = taps
    vert = vert.reshape(len(groups), rows_out // 8, 64, padded_rows).swapaxes(0, 1)
    vert = vert.reshape(rows_out // 8, len(groups) * 64, padded_rows)
    high, low = split_constant(vert)
    vert_stack = np.concatenate([high, high, low], axis=2)
    flat = [taps for filters in groups for taps in filters]
    horiz = np.zeros((2 * LANES, len(flat), LANES))
    for h, taps in enumerate(flat):
        for o in range(LANES):
            start = o + LANES // 2 - HALF
            horiz[start : start + taps.shape[0], h, o] = taps
    horiz_stack = np.stack(split_constant(horiz.reshape(2 * LANES, len(flat) * LANES)))
    place = np.zeros((KERNELS, LANES), np.float32)
    index, base = 0, 0
    for degree in gauss_degrees:
        for a in range(degree + 1):
            for b in range(degree + 1 - a):
                place[index, (base + b) * 8 + a] = 1.0
                index += 1
        base += degree + 1
    return vert_stack, horiz_stack, place


def split(values):
    high = values.astype(jnp.bfloat16)
    return high, (values - high.astype(jnp.float32)).astype(jnp.bfloat16)


def dot32(a, b):
    return jnp.dot(a, b, preferred_element_type=jnp.float32)


def exact(a, b):
    return jnp.dot(a, b, precision=lax.Precision.HIGHEST, preferred_element_type=jnp.float32)


def strip_kernel(
    image_hbm, words_hbm, coef_hbm, order_hbm, place_hbm, vert_hbm, horiz_hbm, out,
    image, words, coef, order, place, sums, got_core, got_y, got_z, ext, valid, vert, horiz, conv, mix, models, got,
    load_sem, const_sem, send_core, recv_core, send_y, recv_y, send_z, recv_z, send_halo, recv_halo, send_model, recv_model,
):
    count = 16
    zs = count // 4
    slab = 2 * LANES
    me = lax.axis_index("epoch")
    k = lax.rem(me, 2)
    y = lax.rem(me // 2, 2)
    z = me // 4

    def remote(src, dst, ssem, rsem, device):
        return pltpu.make_async_remote_copy(
            src_ref=src, dst_ref=dst, send_sem=ssem, recv_sem=rsem,
            device_id={"epoch": device}, device_id_type=pl.DeviceIdType.MESH,
        )

    words_load = pltpu.make_async_copy(words_hbm, words, load_sem.at[0])
    words_load.start()
    loads = []
    for c in range(4):
        part = pl.ds(c * 1024, 1024)
        load = pltpu.make_async_copy(image_hbm.at[:, :, part], image.at[:, :, part], load_sem.at[1 + c])
        load.start()
        loads.append(load)
    barrier = pltpu.get_barrier_semaphore()
    for d in range(1, count):
        pl.semaphore_signal(
            barrier, inc=1, device_id={"epoch": lax.rem(me + d, count)}, device_id_type=pl.DeviceIdType.MESH
        )

    lane = lax.broadcasted_iota(jnp.int32, (8, LANES), 1)
    place_bit = lane & 31
    words_load.wait()
    for q in range(count):
        if q % 4 == 0:
            loads[q // 4].wait()
        for half in range(2):
            t = q * 2 + half
            word = jnp.where(
                lane < 64,
                jnp.where(lane < 32, words[4 * t], words[4 * t + 1]),
                jnp.where(lane < 96, words[4 * t + 2], words[4 * t + 3]),
            )
            bits = (jnp.right_shift(word, place_bit) & 1).astype(jnp.float32)
            valid[:, t * LANES : (t + 1) * LANES] = bits
            spot = sums.at[q % 2, (q // 2) % 2, q // 4]
            for s in range(0, 64, 8):
                spot[s : s + 8, half * LANES : (half + 1) * LANES] = (
                    bits * image[0, s : s + 8, t * LANES : (t + 1) * LANES]
                )
            spot[0:1, half * LANES : (half + 1) * LANES] = bits[0:1]
    pl.semaphore_wait(barrier, count - 1)

    core_copies = []
    for h, yy in enumerate((1 - y, y)):
        copy = remote(
            sums.at[1 - k, yy], got_core.at[yy], send_core.at[h], recv_core.at[h], me + 1 - 2 * k
        )
        copy.start()
        core_copies.append(copy)
    constants = []
    sources = (order_hbm, coef_hbm, place_hbm, vert_hbm, horiz_hbm)
    for c, (src, dst) in enumerate(zip(sources, (order, coef, place, vert, horiz))):
        load = pltpu.make_async_copy(src, dst, const_sem.at[c])
        load.start()
        constants.append(load)
    core_copies[0].wait_recv()
    ring = [lax.rem(z + d, zs) for d in (2, 1, 3, 0)]
    y_copies = []
    for zz in ring:
        sums[k, 1 - y, zz] = sums[k, 1 - y, zz] + got_core[1 - y, zz]
        copy = remote(sums.at[k, 1 - y, zz], got_y.at[zz], send_y.at[zz], recv_y.at[zz], me + 2 - 4 * y)
        copy.start()
        y_copies.append(copy)
    core_copies[1].wait_recv()
    for zz in ring:
        sums[k, y, zz] = sums[k, y, zz] + got_core[y, zz]

    slots = lax.broadcasted_iota(jnp.int32, (count, count), 1)
    for load in constants:
        load.wait()
    rows = lax.broadcasted_iota(jnp.int32, (count, count), 0)
    held = jnp.zeros((count, count), jnp.int32)
    for e in range(count):
        held = jnp.where(rows == e, order[e], held)
    pick = (slots == held).astype(jnp.float32)
    for p in range(POLY):
        table = exact(exact(pick, coef[p]), place[...])
        high, low = split(table)
        rows = slice(p * count, (p + 1) * count)
        mix[rows, :LANES] = high
        mix[rows, LANES:] = high
        rows = slice((POLY + p) * count, (POLY + p + 1) * count)
        mix[rows, :LANES] = low
        mix[rows, LANES:] = jnp.zeros_like(low)

    z_copies = []
    for zz, copy in zip(ring, y_copies):
        copy.wait_recv()
        sums[k, y, zz] = sums[k, y, zz] + got_y[zz]
        if len(z_copies) < zs - 1:
            sent = remote(
                sums.at[k, y, zz], got_z.at[z], send_z.at[zz], recv_z.at[z], zz * 4 + lax.rem(me, 4)
            )
            sent.start()
            z_copies.append(sent)
    for zz in ring[:-1]:
        remote(sums.at[k, y, zz], got_z.at[zz], send_z.at[zz], recv_z.at[zz], me).wait_recv()
    total = sums[k, y, z]
    for zz in ring[:-1]:
        total = total + got_z[zz]
    ext[:, LANES : 3 * LANES] = total / jnp.maximum(total[0:1], 1.0)

    left = lax.rem(me + count - 1, count)
    right = lax.rem(me + 1, count)
    halo = [
        remote(ext.at[:, LANES : 2 * LANES], ext.at[:, 3 * LANES :], send_halo.at[0], recv_halo.at[0], left),
        remote(ext.at[:, 2 * LANES : 3 * LANES], ext.at[:, :LANES], send_halo.at[1], recv_halo.at[1], right),
    ]
    for copy in halo:
        copy.start()
    for copy in halo:
        copy.wait_recv()
    first = jnp.where(me > 0, ext[:, :LANES], 0.0)
    last = jnp.where(me < count - 1, ext[:, 3 * LANES :], 0.0)
    joined = jnp.concatenate([first, ext[:, LANES : 3 * LANES], last], axis=1)
    half = LANES // 2
    windows = jnp.concatenate([joined[:, half : half + slab], joined[:, LANES + half : LANES + half + slab]], axis=1)
    high, low = split(windows)
    stacked = jnp.concatenate([high, low, high], axis=0)
    column = me * slab + lax.broadcasted_iota(jnp.int32, (count, slab), 1)
    across = (2.0 * column.astype(jnp.float32) + 1.0) / (count * slab) - 1.0
    pairs = 15
    rows_out = 32

    def model_rows(blk, carry):
        made = dot32(vert[blk], stacked)
        base = 0
        for g, degree in enumerate(gauss_degrees):
            rows = made[g * 64 : (g + 1) * 64]
            high, low = split(jnp.concatenate([rows[:, :slab], rows[:, slab:]], axis=0))
            outs = slice(base * LANES, (base + degree + 1) * LANES)
            both = dot32(jnp.concatenate([high, low], axis=0), horiz[0, :, outs])
            conv[:, outs] = both[:LANES] + both[LANES:] + dot32(high, horiz[1, :, outs])
            base += degree + 1
        for i in range(8):
            r = blk * 8 + i
            sides = []
            for w in range(2):
                line = slice(w * 64 + i * 8, w * 64 + i * 8 + 8)
                pieces = [conv[line, h * LANES : (h + 1) * LANES] for h in range(pairs)]
                pieces.append(jnp.zeros((8, LANES), jnp.float32))
                sides.append(jnp.concatenate(pieces, axis=0))
            high, low = split(jnp.concatenate(sides, axis=1))
            made = dot32(mix[...], jnp.concatenate([high, low], axis=0))
            made = made[: POLY * count] + made[POLY * count :]
            down = (2.0 * lax.convert_element_type(r, jnp.float32) + 1.0) / rows_out - 1.0
            models[:, r, :] = made[:count] + across * made[count : 2 * count] + down * made[2 * count :]
        start = pl.multiple_of(blk * 8, 8)
        for d in ORDER:
            peer = lax.rem(me + d, count)
            remote(
                models.at[peer, pl.ds(start, 8)], got.at[me, pl.ds(start, 8)],
                send_model.at[blk, peer], recv_model.at[blk, me], peer,
            ).start()
        return carry

    lax.fori_loop(0, rows_out // 8, model_rows, 0)

    def finish(q, source):
        start = pl.multiple_of(q * slab, slab)
        seen = valid[:, pl.ds(start, slab)]
        for s in range(0, rows_out, 8):
            out[0, s : s + 8, pl.ds(start, slab)] = seen * (
                image[0, MARGIN + s : MARGIN + s + 8, pl.ds(start, slab)] - source[q, s : s + 8, :]
            )

    finish(me, models)
    for d in ORDER:
        q = lax.rem(me + count - d, count)
        for blk in range(rows_out // 8):
            rows = pl.ds(blk * 8, 8)
            remote(
                models.at[q, rows], got.at[q, rows], send_model.at[blk, q], recv_model.at[blk, q], q
            ).wait_recv()
        finish(q, got)

    for copy in core_copies + y_copies + z_copies + halo:
        copy.wait_send()
    for d in ORDER:
        peer = lax.rem(me + d, count)
        for blk in range(rows_out // 8):
            rows = pl.ds(blk * 8, 8)
            remote(
                models.at[peer, rows], got.at[me, rows], send_model.at[blk, peer], recv_model.at[blk, me], peer
            ).wait_send()


ORDER = (8, 7, 9, 6, 10, 5, 11, 4, 12, 3, 13, 2, 14, 1, 15)


def strip(epoch_images, mask_words, coefficients, epoch_order):
    vert, horiz, place = kernel_constants(32, 64)
    vmem = pl.BlockSpec(memory_space=pltpu.VMEM)
    hbm = pl.BlockSpec(memory_space=pltpu.HBM)
    f32 = jnp.float32
    bf16 = jnp.bfloat16
    dma = pltpu.SemaphoreType.DMA
    return pl.pallas_call(
        strip_kernel,
        out_shape=jax.ShapeDtypeStruct((1, 32, 4096), f32),
        in_specs=[hbm] * 7,
        out_specs=vmem,
        scratch_shapes=[
            pltpu.VMEM((1, 64, 4096), f32),
            pltpu.SMEM((128,), jnp.int32),
            pltpu.VMEM((3, 16, 49), f32),
            pltpu.SMEM((16,), jnp.int32),
            pltpu.VMEM(place.shape, f32),
            pltpu.VMEM((2, 2, 4, 64, 256), f32),
            pltpu.VMEM((2, 4, 64, 256), f32),
            pltpu.VMEM((4, 64, 256), f32),
            pltpu.VMEM((4, 64, 256), f32),
            pltpu.VMEM((64, 512), f32),
            pltpu.VMEM((8, 4096), f32),
            pltpu.VMEM(vert.shape, bf16),
            pltpu.VMEM(horiz.shape, bf16),
            pltpu.VMEM((128, 15 * LANES), f32),
            pltpu.VMEM((96, 256), bf16),
            pltpu.VMEM((16, 32, 256), f32),
            pltpu.VMEM((16, 32, 256), f32),
            dma((5,)),
            dma((5,)),
            dma((2,)),
            dma((2,)),
            dma((4,)),
            dma((4,)),
            dma((4,)),
            dma((4,)),
            dma((2,)),
            dma((2,)),
            dma((4, 16)),
            dma((4, 16)),
        ],
        compiler_params=pltpu.CompilerParams(
            collective_id=0, has_side_effects=True, vmem_limit_bytes=40 * 1024 * 1024
        ),
        cost_estimate=pl.CostEstimate(flops=2 * 10**9, bytes_accessed=4 * 10**6, transcendentals=0),
    )(
        epoch_images,
        mask_words.reshape(-1),
        jnp.transpose(coefficients, (2, 0, 1)),
        epoch_order,
        jnp.asarray(place),
        jnp.asarray(vert),
        jnp.asarray(horiz),
    )


def solution(mesh):
    placed = (
        P(("patch", "epoch"), None, None),
        P(("patch", "epoch"), None, None),
        P("patch", None, None),
        P("patch"),
    )
    body = strip if mesh.shape["epoch"] == 16 else shards
    return jax.shard_map(
        body,
        mesh=mesh,
        in_specs=placed,
        out_specs=P(("patch", "epoch"), None, None),
        check_vma=False,
    )
```

```python
import math

import jax
import jax.numpy as jnp
import ml_dtypes
import numpy as np
from jax import lax
from jax.experimental import pallas as pl
from jax.experimental.pallas import tpu as pltpu
from jax.sharding import PartitionSpec as P

HALF = 15
MARGIN = 16
BAND = 64
KERNELS = 49
POLY = 3
LANES = 128


gauss_widths = (1.5, 3.0, 6.0)
gauss_degrees = (6, 4, 2)


def extended(cells, sides, width):
    for axis, dim in sides:
        count = lax.axis_size(axis)
        ends = count - 1
        head = lax.slice_in_dim(cells, 0, width, axis=dim)
        tail = lax.slice_in_dim(cells, cells.shape[dim] - width, cells.shape[dim], axis=dim)
        cells = jnp.concatenate(
            [
                lax.ppermute(tail, axis, [(i, (i + 1) % count) for i in range(ends)]),
                cells,
                lax.ppermute(head, axis, [((i + 1) % count, i) for i in range(ends)]),
            ],
            axis=dim,
        )
    return cells


def basis_filters(half_width):
    offsets = jnp.arange(-half_width, half_width + 1).astype(jnp.float32)
    result = []
    for spread_width, degree in zip(gauss_widths, gauss_degrees):
        envelope = jnp.exp(-offsets * offsets / (2.0 * spread_width * spread_width)) / (
            math.sqrt(2.0 * math.pi) * spread_width
        )
        for vert_power in range(degree + 1):
            result.append(envelope * (offsets / spread_width) ** vert_power)
    return jnp.stack(result)


def kernel_pairs():
    result = []
    first_index = 0
    for degree in gauss_degrees:
        for vert_power in range(degree + 1):
            for horiz_power in range(degree + 1 - vert_power):
                result.append((first_index + vert_power, first_index + horiz_power))
        first_index = first_index + degree + 1
    return result


def unpack_valid(mask_words):
    bit_places = jnp.arange(32, dtype=jnp.int32)
    bit_values = jnp.right_shift(mask_words[..., None], bit_places) & 1
    word_shape = mask_words.shape
    return bit_values.reshape(word_shape[0], word_shape[1], word_shape[2] * 32).astype(jnp.float32)


def shift_table(tap_count, inner_cols, outer_cols):
    taps_axis = jnp.arange(tap_count)[:, None, None]
    inner_axis = jnp.arange(inner_cols)[None, :, None]
    outer_axis = jnp.arange(outer_cols)[None, None, :]
    return (inner_axis - outer_axis == taps_axis).astype(jnp.float32)


def vertical_matrices(filters, rows_out, padded_rows):
    tap_count = filters.shape[1]
    out_rows = jnp.arange(rows_out)[:, None]
    in_rows = jnp.arange(padded_rows)[None, :]
    places = in_rows - out_rows - MARGIN + HALF
    one_hot = (places[None] == jnp.arange(tap_count)[:, None, None]).astype(jnp.float32)
    return jnp.einsum("jd,drt->jrt", filters, one_hot, precision=lax.Precision.HIGHEST)


def spatial_terms(col_start, col_count, total_columns, rows_out):
    columns = (
        2.0 * (col_start + jnp.arange(col_count)).astype(jnp.float32) + 1.0
    ) / total_columns - 1.0
    row_pos = (2.0 * jnp.arange(rows_out).astype(jnp.float32) + 1.0) / rows_out - 1.0
    return jnp.stack(
        [
            jnp.ones((rows_out, col_count), jnp.float32),
            jnp.broadcast_to(columns[None, :], (rows_out, col_count)),
            jnp.broadcast_to(row_pos[:, None], (rows_out, col_count)),
        ]
    )


def shards(epoch_images, mask_words, coefficients, epoch_order):
    slot_count, padded_rows, total_columns = epoch_images.shape
    rows_out = padded_rows - 2 * MARGIN
    band_valid = unpack_valid(mask_words)
    valid_mask = jnp.repeat(band_valid, BAND, axis=1)
    part_total = jnp.sum(valid_mask * epoch_images, axis=0)
    part_count = jnp.sum(band_valid, axis=0)
    filters = basis_filters(HALF)
    pair_list = kernel_pairs()
    vert_table = np.zeros((len(pair_list), filters.shape[0]), np.float32)
    horiz_table = np.zeros((len(pair_list), filters.shape[0]), np.float32)
    for kernel_index, pair_value in enumerate(pair_list):
        vert_table[kernel_index, pair_value[0]] = 1.0
        horiz_table[kernel_index, pair_value[1]] = 1.0
    vert_pick = jnp.asarray(vert_table)
    horiz_filters = jnp.dot(jnp.asarray(horiz_table), filters, precision=lax.Precision.HIGHEST)
    vert_mats = vertical_matrices(filters, rows_out, padded_rows)
    full_sum, full_count = (
        lax.psum_scatter(part_total, "epoch", scatter_dimension=1, tiled=True),
        lax.psum_scatter(part_count, "epoch", scatter_dimension=1, tiled=True),
    )
    template = full_sum / jnp.maximum(jnp.repeat(full_count, BAND, axis=0), 1.0)
    slab_cols = template.shape[1]
    rimmed = extended(template, (("epoch", 1),), HALF)
    vertical = jnp.einsum("jrt,tc->jrc", vert_mats, rimmed, precision=lax.Precision.HIGHEST)
    picked = jnp.einsum("kj,jrc->krc", vert_pick, vertical, precision=lax.Precision.HIGHEST)
    horiz_mats = jnp.einsum(
        "kd,dso->kso",
        horiz_filters,
        shift_table(horiz_filters.shape[1], slab_cols + 2 * HALF, slab_cols),
        precision=lax.Precision.HIGHEST,
    )
    convolved = jnp.einsum("krs,kso->kro", picked, horiz_mats, precision=lax.Precision.HIGHEST)
    spatial = spatial_terms(lax.axis_index("epoch") * slab_cols, slab_cols, total_columns, rows_out)
    term_count = coefficients.shape[1] * coefficients.shape[2]
    basis_images = (convolved[:, None] * spatial[None]).reshape(term_count, rows_out * slab_cols)
    coef_table = coefficients[epoch_order].reshape(coefficients.shape[0], term_count)
    models = jnp.dot(
        coef_table,
        basis_images,
        precision=lax.Precision.HIGHEST,
        preferred_element_type=jnp.float32,
    ).reshape(coefficients.shape[0], rows_out, slab_cols)
    model_image = lax.all_to_all(models, "epoch", split_axis=0, concat_axis=2, tiled=True)
    centre = epoch_images[:, MARGIN : MARGIN + rows_out]
    return valid_mask[:, MARGIN : MARGIN + rows_out] * (centre - model_image)


def filter_values():
    offsets = np.arange(-HALF, HALF + 1).astype(np.float64)
    groups = []
    for spread, degree in zip(gauss_widths, gauss_degrees):
        envelope = np.exp(-offsets * offsets / (2.0 * spread * spread)) / (math.sqrt(2.0 * math.pi) * spread)
        groups.append([envelope * (offsets / spread) ** power for power in range(degree + 1)])
    return groups


def split_constant(values):
    values = values.astype(np.float32)
    high = values.astype(ml_dtypes.bfloat16)
    low = (values - high.astype(np.float32)).astype(ml_dtypes.bfloat16)
    return high, low


def kernel_constants(rows_out, padded_rows):
    groups = filter_values()
    vert = np.zeros((len(groups), rows_out, 8, padded_rows))
    for g, filters in enumerate(groups):
        for j, taps in enumerate(filters):
            for r in range(rows_out):
                start = r + MARGIN - HALF
                vert[g, r, j, start : start + taps.shape[0]] = taps
    vert = vert.reshape(len(groups), rows_out // 8, 64, padded_rows).swapaxes(0, 1)
    vert = vert.reshape(rows_out // 8, len(groups) * 64, padded_rows)
    high, low = split_constant(vert)
    vert_stack = np.concatenate([high, high, low], axis=2)
    flat = [taps for filters in groups for taps in filters]
    horiz = np.zeros((2 * LANES, len(flat), LANES))
    for h, taps in enumerate(flat):
        for o in range(LANES):
            start = o + LANES // 2 - HALF
            horiz[start : start + taps.shape[0], h, o] = taps
    horiz_stack = np.stack(split_constant(horiz.reshape(2 * LANES, len(flat) * LANES)))
    place = np.zeros((KERNELS, LANES), np.float32)
    index, base = 0, 0
    for degree in gauss_degrees:
        for a in range(degree + 1):
            for b in range(degree + 1 - a):
                place[index, (base + b) * 8 + a] = 1.0
                index += 1
        base += degree + 1
    return vert_stack, horiz_stack, place


def split(values):
    high = values.astype(jnp.bfloat16)
    return high, (values - high.astype(jnp.float32)).astype(jnp.bfloat16)


def dot32(a, b):
    return jnp.dot(a, b, preferred_element_type=jnp.float32)


def exact(a, b):
    return jnp.dot(a, b, precision=lax.Precision.HIGHEST, preferred_element_type=jnp.float32)


def strip_kernel(
    image_hbm, words_hbm, coef_hbm, order_hbm, place_hbm, vert_hbm, horiz_hbm, out,
    image, words, coef, order, place, sums, got_core, got_y, got_z, ext, valid, vert, horiz, conv, mix, models, got,
    load_sem, const_sem, send_core, recv_core, send_y, recv_y, send_z, recv_z, send_halo, recv_halo, send_model, recv_model,
):
    count = 16
    zs = count // 4
    slab = 2 * LANES
    me = lax.axis_index("epoch")
    k = lax.rem(me, 2)
    y = lax.rem(me // 2, 2)
    z = me // 4

    def remote(src, dst, ssem, rsem, device):
        return pltpu.make_async_remote_copy(
            src_ref=src, dst_ref=dst, send_sem=ssem, recv_sem=rsem,
            device_id={"epoch": device}, device_id_type=pl.DeviceIdType.MESH,
        )

    words_load = pltpu.make_async_copy(words_hbm, words, load_sem.at[0])
    words_load.start()
    loads = []
    for c in range(4):
        part = pl.ds(c * 1024, 1024)
        load = pltpu.make_async_copy(image_hbm.at[:, :, part], image.at[:, :, part], load_sem.at[1 + c])
        load.start()
        loads.append(load)
    barrier = pltpu.get_barrier_semaphore()
    for d in range(1, count):
        pl.semaphore_signal(
            barrier, inc=1, device_id={"epoch": lax.rem(me + d, count)}, device_id_type=pl.DeviceIdType.MESH
        )

    lane = lax.broadcasted_iota(jnp.int32, (8, LANES), 1)
    place_bit = lane & 31
    words_load.wait()
    for q in range(count):
        if q % 4 == 0:
            loads[q // 4].wait()
        for half in range(2):
            t = q * 2 + half
            word = jnp.where(
                lane < 64,
                jnp.where(lane < 32, words[4 * t], words[4 * t + 1]),
                jnp.where(lane < 96, words[4 * t + 2], words[4 * t + 3]),
            )
            bits = (jnp.right_shift(word, place_bit) & 1).astype(jnp.float32)
            valid[:, t * LANES : (t + 1) * LANES] = bits
            spot = sums.at[q % 2, (q // 2) % 2, q // 4]
            for s in range(0, 64, 8):
                spot[s : s + 8, half * LANES : (half + 1) * LANES] = (
                    bits * image[0, s : s + 8, t * LANES : (t + 1) * LANES]
                )
            spot[0:1, half * LANES : (half + 1) * LANES] = bits[0:1]
    pl.semaphore_wait(barrier, count - 1)

    core_copies = []
    for h, yy in enumerate((1 - y, y)):
        copy = remote(
            sums.at[1 - k, yy], got_core.at[yy], send_core.at[h], recv_core.at[h], me + 1 - 2 * k
        )
        copy.start()
        core_copies.append(copy)
    constants = []
    sources = (order_hbm, coef_hbm, place_hbm, vert_hbm, horiz_hbm)
    for c, (src, dst) in enumerate(zip(sources, (order, coef, place, vert, horiz))):
        load = pltpu.make_async_copy(src, dst, const_sem.at[c])
        load.start()
        constants.append(load)
    core_copies[0].wait_recv()
    ring = [lax.rem(z + d, zs) for d in (2, 1, 3, 0)]
    y_copies = []
    for zz in ring:
        sums[k, 1 - y, zz] = sums[k, 1 - y, zz] + got_core[1 - y, zz]
        copy = remote(sums.at[k, 1 - y, zz], got_y.at[zz], send_y.at[zz], recv_y.at[zz], me + 2 - 4 * y)
        copy.start()
        y_copies.append(copy)
    core_copies[1].wait_recv()
    for zz in ring:
        sums[k, y, zz] = sums[k, y, zz] + got_core[y, zz]

    slots = lax.broadcasted_iota(jnp.int32, (count, count), 1)
    for load in constants:
        load.wait()
    rows = lax.broadcasted_iota(jnp.int32, (count, count), 0)
    held = jnp.zeros((count, count), jnp.int32)
    for e in range(count):
        held = jnp.where(rows == e, order[e], held)
    pick = (slots == held).astype(jnp.float32)
    for p in range(POLY):
        table = exact(exact(pick, coef[p]), place[...])
        high, low = split(table)
        rows = slice(p * count, (p + 1) * count)
        mix[rows, :LANES] = high
        mix[rows, LANES:] = high
        rows = slice((POLY + p) * count, (POLY + p + 1) * count)
        mix[rows, :LANES] = low
        mix[rows, LANES:] = jnp.zeros_like(low)

    z_copies = []
    for zz, copy in zip(ring, y_copies):
        copy.wait_recv()
        sums[k, y, zz] = sums[k, y, zz] + got_y[zz]
        if len(z_copies) < zs - 1:
            sent = remote(
                sums.at[k, y, zz], got_z.at[z], send_z.at[zz], recv_z.at[z], zz * 4 + lax.rem(me, 4)
            )
            sent.start()
            z_copies.append(sent)
    for zz in ring[:-1]:
        remote(sums.at[k, y, zz], got_z.at[zz], send_z.at[zz], recv_z.at[zz], me).wait_recv()
    total = sums[k, y, z]
    for zz in ring[:-1]:
        total = total + got_z[zz]
    ext[:, LANES : 3 * LANES] = total / jnp.maximum(total[0:1], 1.0)

    left = lax.rem(me + count - 1, count)
    right = lax.rem(me + 1, count)
    halo = [
        remote(ext.at[:, LANES : 2 * LANES], ext.at[:, 3 * LANES :], send_halo.at[0], recv_halo.at[0], left),
        remote(ext.at[:, 2 * LANES : 3 * LANES], ext.at[:, :LANES], send_halo.at[1], recv_halo.at[1], right),
    ]
    for copy in halo:
        copy.start()
    for copy in halo:
        copy.wait_recv()
    first = jnp.where(me > 0, ext[:, :LANES], 0.0)
    last = jnp.where(me < count - 1, ext[:, 3 * LANES :], 0.0)
    joined = jnp.concatenate([first, ext[:, LANES : 3 * LANES], last], axis=1)
    half = LANES // 2
    windows = jnp.concatenate([joined[:, half : half + slab], joined[:, LANES + half : LANES + half + slab]], axis=1)
    high, low = split(windows)
    stacked = jnp.concatenate([high, low, high], axis=0)
    column = me * slab + lax.broadcasted_iota(jnp.int32, (count, slab), 1)
    across = (2.0 * column.astype(jnp.float32) + 1.0) / (count * slab) - 1.0
    pairs = 15
    rows_out = 32

    def model_rows(blk, carry):
        made = dot32(vert[blk], stacked)
        base = 0
        for g, degree in enumerate(gauss_degrees):
            rows = made[g * 64 : (g + 1) * 64]
            high, low = split(jnp.concatenate([rows[:, :slab], rows[:, slab:]], axis=0))
            outs = slice(base * LANES, (base + degree + 1) * LANES)
            both = dot32(jnp.concatenate([high, low], axis=0), horiz[0, :, outs])
            conv[:, outs] = both[:LANES] + both[LANES:] + dot32(high, horiz[1, :, outs])
            base += degree + 1
        for i in range(8):
            r = blk * 8 + i
            sides = []
            for w in range(2):
                line = slice(w * 64 + i * 8, w * 64 + i * 8 + 8)
                pieces = [conv[line, h * LANES : (h + 1) * LANES] for h in range(pairs)]
                pieces.append(jnp.zeros((8, LANES), jnp.float32))
                sides.append(jnp.concatenate(pieces, axis=0))
            high, low = split(jnp.concatenate(sides, axis=1))
            made = dot32(mix[...], jnp.concatenate([high, low], axis=0))
            made = made[: POLY * count] + made[POLY * count :]
            down = (2.0 * lax.convert_element_type(r, jnp.float32) + 1.0) / rows_out - 1.0
            models[:, r, :] = made[:count] + across * made[count : 2 * count] + down * made[2 * count :]
        start = pl.multiple_of(blk * 8, 8)
        for d in ORDER:
            peer = lax.rem(me + d, count)
            remote(
                models.at[peer, pl.ds(start, 8)], got.at[me, pl.ds(start, 8)],
                send_model.at[blk, peer], recv_model.at[blk, me], peer,
            ).start()
        return carry

    lax.fori_loop(0, rows_out // 8, model_rows, 0)

    def finish(q, source):
        start = pl.multiple_of(q * slab, slab)
        seen = valid[:, pl.ds(start, slab)]
        for s in range(0, rows_out, 8):
            out[0, s : s + 8, pl.ds(start, slab)] = seen * (
                image[0, MARGIN + s : MARGIN + s + 8, pl.ds(start, slab)] - source[q, s : s + 8, :]
            )

    finish(me, models)
    for d in ORDER:
        q = lax.rem(me + count - d, count)
        for blk in range(rows_out // 8):
            rows = pl.ds(blk * 8, 8)
            remote(
                models.at[q, rows], got.at[q, rows], send_model.at[blk, q], recv_model.at[blk, q], q
            ).wait_recv()
        finish(q, got)

    for copy in core_copies + y_copies + z_copies + halo:
        copy.wait_send()
    for d in ORDER:
        peer = lax.rem(me + d, count)
        for blk in range(rows_out // 8):
            rows = pl.ds(blk * 8, 8)
            remote(
                models.at[peer, rows], got.at[me, rows], send_model.at[blk, peer], recv_model.at[blk, me], peer
            ).wait_send()


ORDER = (8, 7, 9, 6, 10, 5, 11, 4, 12, 3, 13, 2, 14, 1, 15)


def strip(epoch_images, mask_words, coefficients, epoch_order):
    vert, horiz, place = kernel_constants(32, 64)
    vmem = pl.BlockSpec(memory_space=pltpu.VMEM)
    hbm = pl.BlockSpec(memory_space=pltpu.HBM)
    f32 = jnp.float32
    bf16 = jnp.bfloat16
    dma = pltpu.SemaphoreType.DMA
    return pl.pallas_call(
        strip_kernel,
        out_shape=jax.ShapeDtypeStruct((1, 32, 4096), f32),
        in_specs=[hbm] * 7,
        out_specs=vmem,
        scratch_shapes=[
            pltpu.VMEM((1, 64, 4096), f32),
            pltpu.SMEM((128,), jnp.int32),
            pltpu.VMEM((3, 16, 49), f32),
            pltpu.SMEM((16,), jnp.int32),
            pltpu.VMEM(place.shape, f32),
            pltpu.VMEM((2, 2, 4, 64, 256), f32),
            pltpu.VMEM((2, 4, 64, 256), f32),
            pltpu.VMEM((4, 64, 256), f32),
            pltpu.VMEM((4, 64, 256), f32),
            pltpu.VMEM((64, 512), f32),
            pltpu.VMEM((8, 4096), f32),
            pltpu.VMEM(vert.shape, bf16),
            pltpu.VMEM(horiz.shape, bf16),
            pltpu.VMEM((128, 15 * LANES), f32),
            pltpu.VMEM((96, 256), bf16),
            pltpu.VMEM((16, 32, 256), f32),
            pltpu.VMEM((16, 32, 256), f32),
            dma((5,)),
            dma((5,)),
            dma((2,)),
            dma((2,)),
            dma((4,)),
            dma((4,)),
            dma((4,)),
            dma((4,)),
            dma((2,)),
            dma((2,)),
            dma((4, 16)),
            dma((4, 16)),
        ],
        compiler_params=pltpu.CompilerParams(
            collective_id=0, has_side_effects=True, vmem_limit_bytes=64 * 1024 * 1024 - 4096
        ),
        cost_estimate=pl.CostEstimate(flops=2 * 10**9, bytes_accessed=4 * 10**6, transcendentals=0),
    )(
        epoch_images,
        mask_words.reshape(-1),
        jnp.transpose(coefficients, (2, 0, 1)),
        epoch_order,
        jnp.asarray(place),
        jnp.asarray(vert),
        jnp.asarray(horiz),
    )


def solution(mesh):
    placed = (
        P(("patch", "epoch"), None, None),
        P(("patch", "epoch"), None, None),
        P("patch", None, None),
        P("patch"),
    )
    body = strip if mesh.shape["epoch"] == 16 else shards
    return jax.shard_map(
        body,
        mesh=mesh,
        in_specs=placed,
        out_specs=P(("patch", "epoch"), None, None),
        check_vma=False,
    )
```

```python
import math

import jax
import jax.numpy as jnp
import ml_dtypes
import numpy as np
from jax import lax
from jax.experimental import pallas as pl
from jax.experimental.pallas import tpu as pltpu
from jax.sharding import PartitionSpec as P

HALF = 15
MARGIN = 16
BAND = 64
KERNELS = 49
POLY = 3
LANES = 128
PIECE = 16


gauss_widths = (1.5, 3.0, 6.0)
gauss_degrees = (6, 4, 2)


def extended(cells, sides, width):
    for axis, dim in sides:
        count = lax.axis_size(axis)
        ends = count - 1
        head = lax.slice_in_dim(cells, 0, width, axis=dim)
        tail = lax.slice_in_dim(cells, cells.shape[dim] - width, cells.shape[dim], axis=dim)
        cells = jnp.concatenate(
            [
                lax.ppermute(tail, axis, [(i, (i + 1) % count) for i in range(ends)]),
                cells,
                lax.ppermute(head, axis, [((i + 1) % count, i) for i in range(ends)]),
            ],
            axis=dim,
        )
    return cells


def basis_filters(half_width):
    offsets = jnp.arange(-half_width, half_width + 1).astype(jnp.float32)
    result = []
    for spread_width, degree in zip(gauss_widths, gauss_degrees):
        envelope = jnp.exp(-offsets * offsets / (2.0 * spread_width * spread_width)) / (
            math.sqrt(2.0 * math.pi) * spread_width
        )
        for vert_power in range(degree + 1):
            result.append(envelope * (offsets / spread_width) ** vert_power)
    return jnp.stack(result)


def kernel_pairs():
    result = []
    first_index = 0
    for degree in gauss_degrees:
        for vert_power in range(degree + 1):
            for horiz_power in range(degree + 1 - vert_power):
                result.append((first_index + vert_power, first_index + horiz_power))
        first_index = first_index + degree + 1
    return result


def unpack_valid(mask_words):
    bit_places = jnp.arange(32, dtype=jnp.int32)
    bit_values = jnp.right_shift(mask_words[..., None], bit_places) & 1
    word_shape = mask_words.shape
    return bit_values.reshape(word_shape[0], word_shape[1], word_shape[2] * 32).astype(jnp.float32)


def shift_table(tap_count, inner_cols, outer_cols):
    taps_axis = jnp.arange(tap_count)[:, None, None]
    inner_axis = jnp.arange(inner_cols)[None, :, None]
    outer_axis = jnp.arange(outer_cols)[None, None, :]
    return (inner_axis - outer_axis == taps_axis).astype(jnp.float32)


def vertical_matrices(filters, rows_out, padded_rows):
    tap_count = filters.shape[1]
    out_rows = jnp.arange(rows_out)[:, None]
    in_rows = jnp.arange(padded_rows)[None, :]
    places = in_rows - out_rows - MARGIN + HALF
    one_hot = (places[None] == jnp.arange(tap_count)[:, None, None]).astype(jnp.float32)
    return jnp.einsum("jd,drt->jrt", filters, one_hot, precision=lax.Precision.HIGHEST)


def spatial_terms(col_start, col_count, total_columns, rows_out):
    columns = (
        2.0 * (col_start + jnp.arange(col_count)).astype(jnp.float32) + 1.0
    ) / total_columns - 1.0
    row_pos = (2.0 * jnp.arange(rows_out).astype(jnp.float32) + 1.0) / rows_out - 1.0
    return jnp.stack(
        [
            jnp.ones((rows_out, col_count), jnp.float32),
            jnp.broadcast_to(columns[None, :], (rows_out, col_count)),
            jnp.broadcast_to(row_pos[:, None], (rows_out, col_count)),
        ]
    )


def shards(epoch_images, mask_words, coefficients, epoch_order):
    slot_count, padded_rows, total_columns = epoch_images.shape
    rows_out = padded_rows - 2 * MARGIN
    band_valid = unpack_valid(mask_words)
    valid_mask = jnp.repeat(band_valid, BAND, axis=1)
    part_total = jnp.sum(valid_mask * epoch_images, axis=0)
    part_count = jnp.sum(band_valid, axis=0)
    filters = basis_filters(HALF)
    pair_list = kernel_pairs()
    vert_table = np.zeros((len(pair_list), filters.shape[0]), np.float32)
    horiz_table = np.zeros((len(pair_list), filters.shape[0]), np.float32)
    for kernel_index, pair_value in enumerate(pair_list):
        vert_table[kernel_index, pair_value[0]] = 1.0
        horiz_table[kernel_index, pair_value[1]] = 1.0
    vert_pick = jnp.asarray(vert_table)
    horiz_filters = jnp.dot(jnp.asarray(horiz_table), filters, precision=lax.Precision.HIGHEST)
    vert_mats = vertical_matrices(filters, rows_out, padded_rows)
    full_sum, full_count = (
        lax.psum_scatter(part_total, "epoch", scatter_dimension=1, tiled=True),
        lax.psum_scatter(part_count, "epoch", scatter_dimension=1, tiled=True),
    )
    template = full_sum / jnp.maximum(jnp.repeat(full_count, BAND, axis=0), 1.0)
    slab_cols = template.shape[1]
    rimmed = extended(template, (("epoch", 1),), HALF)
    vertical = jnp.einsum("jrt,tc->jrc", vert_mats, rimmed, precision=lax.Precision.HIGHEST)
    picked = jnp.einsum("kj,jrc->krc", vert_pick, vertical, precision=lax.Precision.HIGHEST)
    horiz_mats = jnp.einsum(
        "kd,dso->kso",
        horiz_filters,
        shift_table(horiz_filters.shape[1], slab_cols + 2 * HALF, slab_cols),
        precision=lax.Precision.HIGHEST,
    )
    convolved = jnp.einsum("krs,kso->kro", picked, horiz_mats, precision=lax.Precision.HIGHEST)
    spatial = spatial_terms(lax.axis_index("epoch") * slab_cols, slab_cols, total_columns, rows_out)
    term_count = coefficients.shape[1] * coefficients.shape[2]
    basis_images = (convolved[:, None] * spatial[None]).reshape(term_count, rows_out * slab_cols)
    coef_table = coefficients[epoch_order].reshape(coefficients.shape[0], term_count)
    models = jnp.dot(
        coef_table,
        basis_images,
        precision=lax.Precision.HIGHEST,
        preferred_element_type=jnp.float32,
    ).reshape(coefficients.shape[0], rows_out, slab_cols)
    model_image = lax.all_to_all(models, "epoch", split_axis=0, concat_axis=2, tiled=True)
    centre = epoch_images[:, MARGIN : MARGIN + rows_out]
    return valid_mask[:, MARGIN : MARGIN + rows_out] * (centre - model_image)


def filter_values():
    offsets = np.arange(-HALF, HALF + 1).astype(np.float64)
    groups = []
    for spread, degree in zip(gauss_widths, gauss_degrees):
        envelope = np.exp(-offsets * offsets / (2.0 * spread * spread)) / (math.sqrt(2.0 * math.pi) * spread)
        groups.append([envelope * (offsets / spread) ** power for power in range(degree + 1)])
    return groups


def split_constant(values):
    values = values.astype(np.float32)
    high = values.astype(ml_dtypes.bfloat16)
    low = (values - high.astype(np.float32)).astype(ml_dtypes.bfloat16)
    return high, low


def kernel_constants(rows_out, padded_rows):
    groups = filter_values()
    vert = np.zeros((len(groups), rows_out, 8, padded_rows))
    for g, filters in enumerate(groups):
        for j, taps in enumerate(filters):
            for r in range(rows_out):
                start = r + MARGIN - HALF
                vert[g, r, j, start : start + taps.shape[0]] = taps
    vert = vert.reshape(len(groups), rows_out // PIECE, 8 * PIECE, padded_rows).swapaxes(0, 1)
    vert = vert.reshape(rows_out // PIECE, len(groups) * 8 * PIECE, padded_rows)
    high, low = split_constant(vert)
    vert_stack = np.concatenate([high, high, low], axis=2)
    flat = [taps for filters in groups for taps in filters]
    horiz = np.zeros((2 * LANES, len(flat), LANES))
    for h, taps in enumerate(flat):
        for o in range(LANES):
            start = o + LANES // 2 - HALF
            horiz[start : start + taps.shape[0], h, o] = taps
    horiz_stack = np.stack(split_constant(horiz.reshape(2 * LANES, len(flat) * LANES)))
    place = np.zeros((KERNELS, LANES), np.float32)
    index, base = 0, 0
    for degree in gauss_degrees:
        for a in range(degree + 1):
            for b in range(degree + 1 - a):
                place[index, (base + b) * 8 + a] = 1.0
                index += 1
        base += degree + 1
    return vert_stack, horiz_stack, place


def split(values):
    high = values.astype(jnp.bfloat16)
    return high, (values - high.astype(jnp.float32)).astype(jnp.bfloat16)


def dot32(a, b):
    return jnp.dot(a, b, preferred_element_type=jnp.float32)


def exact(a, b):
    return jnp.dot(a, b, precision=lax.Precision.HIGHEST, preferred_element_type=jnp.float32)


def strip_kernel(
    image_hbm, words_hbm, coef_hbm, order_hbm, place_hbm, vert_hbm, horiz_hbm, out, valid,
    image, words, coef, order, place, sums, got_core, got_y, got_z, ext, vert, horiz, conv, mix, models, got,
    load_sem, const_sem, send_core, recv_core, send_y, recv_y, send_z, recv_z, send_halo, recv_halo, send_model, recv_model,
):
    count = 16
    zs = count // 4
    slab = 2 * LANES
    me = lax.axis_index("epoch")
    k = lax.rem(me, 2)
    y = lax.rem(me // 2, 2)
    z = me // 4

    def remote(src, dst, ssem, rsem, device):
        return pltpu.make_async_remote_copy(
            src_ref=src, dst_ref=dst, send_sem=ssem, recv_sem=rsem,
            device_id={"epoch": device}, device_id_type=pl.DeviceIdType.MESH,
        )

    words_load = pltpu.make_async_copy(words_hbm, words, load_sem.at[0])
    words_load.start()
    loads = []
    for c in range(4):
        part = pl.ds(c * 1024, 1024)
        load = pltpu.make_async_copy(image_hbm.at[:, :, part], image.at[:, :, part], load_sem.at[1 + c])
        load.start()
        loads.append(load)
    barrier = pltpu.get_barrier_semaphore()
    for d in range(1, count):
        pl.semaphore_signal(
            barrier, inc=1, device_id={"epoch": lax.rem(me + d, count)}, device_id_type=pl.DeviceIdType.MESH
        )

    lane = lax.broadcasted_iota(jnp.int32, (8, LANES), 1)
    place_bit = lane & 31
    words_load.wait()
    for q in range(count):
        if q % 4 == 0:
            loads[q // 4].wait()
        for half in range(2):
            t = q * 2 + half
            word = jnp.where(
                lane < 64,
                jnp.where(lane < 32, words[4 * t], words[4 * t + 1]),
                jnp.where(lane < 96, words[4 * t + 2], words[4 * t + 3]),
            )
            bits = (jnp.right_shift(word, place_bit) & 1).astype(jnp.float32)
            valid[:, t * LANES : (t + 1) * LANES] = bits[0:1]
            spot = sums.at[q % 2, (q // 2) % 2, q // 4]
            for s in range(0, 64, 8):
                spot[s : s + 8, half * LANES : (half + 1) * LANES] = (
                    bits * image[0, s : s + 8, t * LANES : (t + 1) * LANES]
                )
            spot[0:1, half * LANES : (half + 1) * LANES] = bits[0:1]
    pl.semaphore_wait(barrier, count - 1)

    core_copies = []
    for h, yy in enumerate((1 - y, y)):
        copy = remote(
            sums.at[1 - k, yy], got_core.at[yy], send_core.at[h], recv_core.at[h], me + 1 - 2 * k
        )
        copy.start()
        core_copies.append(copy)
    constants = []
    sources = (order_hbm, coef_hbm, place_hbm, vert_hbm, horiz_hbm)
    for c, (src, dst) in enumerate(zip(sources, (order, coef, place, vert, horiz))):
        load = pltpu.make_async_copy(src, dst, const_sem.at[c])
        load.start()
        constants.append(load)
    core_copies[0].wait_recv()
    ring = [lax.rem(z + d, zs) for d in (2, 1, 3, 0)]
    y_copies = []
    for zz in ring:
        sums[k, 1 - y, zz] = sums[k, 1 - y, zz] + got_core[1 - y, zz]
        copy = remote(sums.at[k, 1 - y, zz], got_y.at[zz], send_y.at[zz], recv_y.at[zz], me + 2 - 4 * y)
        copy.start()
        y_copies.append(copy)
    core_copies[1].wait_recv()
    for zz in ring:
        sums[k, y, zz] = sums[k, y, zz] + got_core[y, zz]

    slots = lax.broadcasted_iota(jnp.int32, (count, count), 1)
    for load in constants:
        load.wait()
    rows = lax.broadcasted_iota(jnp.int32, (count, count), 0)
    held = jnp.zeros((count, count), jnp.int32)
    for e in range(count):
        held = jnp.where(rows == e, order[e], held)
    pick = (slots == held).astype(jnp.float32)
    for p in range(POLY):
        table = exact(exact(pick, coef[p]), place[...])
        high, low = split(table)
        rows = slice(p * count, (p + 1) * count)
        mix[rows, :LANES] = high
        mix[rows, LANES:] = high
        rows = slice((POLY + p) * count, (POLY + p + 1) * count)
        mix[rows, :LANES] = low
        mix[rows, LANES:] = jnp.zeros_like(low)

    z_copies = []
    for zz, copy in zip(ring, y_copies):
        copy.wait_recv()
        sums[k, y, zz] = sums[k, y, zz] + got_y[zz]
        if len(z_copies) < zs - 1:
            sent = remote(
                sums.at[k, y, zz], got_z.at[z], send_z.at[zz], recv_z.at[z], zz * 4 + lax.rem(me, 4)
            )
            sent.start()
            z_copies.append(sent)
    for zz in ring[:-1]:
        remote(sums.at[k, y, zz], got_z.at[zz], send_z.at[zz], recv_z.at[zz], me).wait_recv()
    total = sums[k, y, z]
    for zz in ring[:-1]:
        total = total + got_z[zz]
    ext[:, LANES : 3 * LANES] = total / jnp.maximum(total[0:1], 1.0)

    left = lax.rem(me + count - 1, count)
    right = lax.rem(me + 1, count)
    halo = [
        remote(ext.at[:, LANES : 2 * LANES], ext.at[:, 3 * LANES :], send_halo.at[0], recv_halo.at[0], left),
        remote(ext.at[:, 2 * LANES : 3 * LANES], ext.at[:, :LANES], send_halo.at[1], recv_halo.at[1], right),
    ]
    for copy in halo:
        copy.start()
    for copy in halo:
        copy.wait_recv()
    first = jnp.where(me > 0, ext[:, :LANES], 0.0)
    last = jnp.where(me < count - 1, ext[:, 3 * LANES :], 0.0)
    joined = jnp.concatenate([first, ext[:, LANES : 3 * LANES], last], axis=1)
    half = LANES // 2
    windows = jnp.concatenate([joined[:, half : half + slab], joined[:, LANES + half : LANES + half + slab]], axis=1)
    high, low = split(windows)
    stacked = jnp.concatenate([high, low, high], axis=0)
    column = me * slab + lax.broadcasted_iota(jnp.int32, (count, slab), 1)
    across = (2.0 * column.astype(jnp.float32) + 1.0) / (count * slab) - 1.0
    pairs = 15
    rows_out = 32

    def model_rows(blk, carry):
        made = dot32(vert[blk], stacked)
        base = 0
        for g, degree in enumerate(gauss_degrees):
            rows = made[g * 8 * PIECE : (g + 1) * 8 * PIECE]
            high, low = split(jnp.concatenate([rows[:, :slab], rows[:, slab:]], axis=0))
            outs = slice(base * LANES, (base + degree + 1) * LANES)
            both = dot32(jnp.concatenate([high, low], axis=0), horiz[0, :, outs])
            conv[:, outs] = both[: 16 * PIECE] + both[16 * PIECE :] + dot32(high, horiz[1, :, outs])
            base += degree + 1
        for i in range(PIECE):
            r = blk * PIECE + i
            sides = []
            for w in range(2):
                line = slice((w * PIECE + i) * 8, (w * PIECE + i + 1) * 8)
                pieces = [conv[line, h * LANES : (h + 1) * LANES] for h in range(pairs)]
                pieces.append(jnp.zeros((8, LANES), jnp.float32))
                sides.append(jnp.concatenate(pieces, axis=0))
            high, low = split(jnp.concatenate(sides, axis=1))
            made = dot32(mix[...], jnp.concatenate([high, low], axis=0))
            made = made[: POLY * count] + made[POLY * count :]
            down = (2.0 * lax.convert_element_type(r, jnp.float32) + 1.0) / rows_out - 1.0
            models[:, r, :] = made[:count] + across * made[count : 2 * count] + down * made[2 * count :]
        start = pl.multiple_of(blk * PIECE, PIECE)
        for d in ORDER:
            peer = lax.rem(me + d, count)
            remote(
                models.at[peer, pl.ds(start, PIECE)], got.at[me, pl.ds(start, PIECE)],
                send_model.at[blk, peer], recv_model.at[blk, me], peer,
            ).start()
        return carry

    lax.fori_loop(0, rows_out // PIECE, model_rows, 0)

    def finish(q, source):
        start = pl.multiple_of(q * slab, slab)
        out[0, :, pl.ds(start, slab)] = source[q]

    finish(me, models)
    for d in ORDER:
        q = lax.rem(me + count - d, count)
        for blk in range(rows_out // PIECE):
            rows = pl.ds(blk * PIECE, PIECE)
            remote(
                models.at[q, rows], got.at[q, rows], send_model.at[blk, q], recv_model.at[blk, q], q
            ).wait_recv()
        finish(q, got)

    for copy in core_copies + y_copies + z_copies + halo:
        copy.wait_send()
    for d in ORDER:
        peer = lax.rem(me + d, count)
        for blk in range(rows_out // PIECE):
            rows = pl.ds(blk * PIECE, PIECE)
            remote(
                models.at[peer, rows], got.at[me, rows], send_model.at[blk, peer], recv_model.at[blk, me], peer
            ).wait_send()


ORDER = (8, 7, 9, 6, 10, 5, 11, 4, 12, 3, 13, 2, 14, 1, 15)


def strip(epoch_images, mask_words, coefficients, epoch_order):
    vert, horiz, place = kernel_constants(32, 64)
    vmem = pl.BlockSpec(memory_space=pltpu.VMEM)
    hbm = pl.BlockSpec(memory_space=pltpu.HBM)
    f32 = jnp.float32
    bf16 = jnp.bfloat16
    dma = pltpu.SemaphoreType.DMA
    model, seen = pl.pallas_call(
        strip_kernel,
        out_shape=[jax.ShapeDtypeStruct((1, 32, 4096), f32), jax.ShapeDtypeStruct((1, 4096), f32)],
        in_specs=[hbm] * 7,
        out_specs=[vmem, vmem],
        scratch_shapes=[
            pltpu.VMEM((1, 64, 4096), f32),
            pltpu.SMEM((128,), jnp.int32),
            pltpu.VMEM((3, 16, 49), f32),
            pltpu.SMEM((16,), jnp.int32),
            pltpu.VMEM(place.shape, f32),
            pltpu.VMEM((2, 2, 4, 64, 256), f32),
            pltpu.VMEM((2, 4, 64, 256), f32),
            pltpu.VMEM((4, 64, 256), f32),
            pltpu.VMEM((4, 64, 256), f32),
            pltpu.VMEM((64, 512), f32),
            pltpu.VMEM(vert.shape, bf16),
            pltpu.VMEM(horiz.shape, bf16),
            pltpu.VMEM((16 * PIECE, 15 * LANES), f32),
            pltpu.VMEM((96, 256), bf16),
            pltpu.VMEM((16, 32, 256), f32),
            pltpu.VMEM((16, 32, 256), f32),
            dma((5,)),
            dma((5,)),
            dma((2,)),
            dma((2,)),
            dma((4,)),
            dma((4,)),
            dma((4,)),
            dma((4,)),
            dma((2,)),
            dma((2,)),
            dma((32 // PIECE, 16)),
            dma((32 // PIECE, 16)),
        ],
        compiler_params=pltpu.CompilerParams(
            collective_id=0, has_side_effects=True, vmem_limit_bytes=64 * 1024 * 1024 - 4096
        ),
        cost_estimate=pl.CostEstimate(flops=2 * 10**9, bytes_accessed=4 * 10**6, transcendentals=0),
    )(
        epoch_images,
        mask_words.reshape(-1),
        jnp.transpose(coefficients, (2, 0, 1)),
        epoch_order,
        jnp.asarray(place),
        jnp.asarray(vert),
        jnp.asarray(horiz),
    )
    return seen[None] * (epoch_images[:, MARGIN : MARGIN + 32] - model)


def solution(mesh):
    placed = (
        P(("patch", "epoch"), None, None),
        P(("patch", "epoch"), None, None),
        P("patch", None, None),
        P("patch"),
    )
    body = strip if mesh.shape["epoch"] == 16 else shards
    return jax.shard_map(
        body,
        mesh=mesh,
        in_specs=placed,
        out_specs=P(("patch", "epoch"), None, None),
        check_vma=False,
    )
```

```python
import math

import jax
import jax.numpy as jnp
import ml_dtypes
import numpy as np
from jax import lax
from jax.experimental import pallas as pl
from jax.experimental.pallas import tpu as pltpu
from jax.sharding import PartitionSpec as P

HALF = 15
MARGIN = 16
BAND = 64
KERNELS = 49
POLY = 3
LANES = 128
PIECE = 16


gauss_widths = (1.5, 3.0, 6.0)
gauss_degrees = (6, 4, 2)


def extended(cells, sides, width):
    for axis, dim in sides:
        count = lax.axis_size(axis)
        ends = count - 1
        head = lax.slice_in_dim(cells, 0, width, axis=dim)
        tail = lax.slice_in_dim(cells, cells.shape[dim] - width, cells.shape[dim], axis=dim)
        cells = jnp.concatenate(
            [
                lax.ppermute(tail, axis, [(i, (i + 1) % count) for i in range(ends)]),
                cells,
                lax.ppermute(head, axis, [((i + 1) % count, i) for i in range(ends)]),
            ],
            axis=dim,
        )
    return cells


def basis_filters(half_width):
    offsets = jnp.arange(-half_width, half_width + 1).astype(jnp.float32)
    result = []
    for spread_width, degree in zip(gauss_widths, gauss_degrees):
        envelope = jnp.exp(-offsets * offsets / (2.0 * spread_width * spread_width)) / (
            math.sqrt(2.0 * math.pi) * spread_width
        )
        for vert_power in range(degree + 1):
            result.append(envelope * (offsets / spread_width) ** vert_power)
    return jnp.stack(result)


def kernel_pairs():
    result = []
    first_index = 0
    for degree in gauss_degrees:
        for vert_power in range(degree + 1):
            for horiz_power in range(degree + 1 - vert_power):
                result.append((first_index + vert_power, first_index + horiz_power))
        first_index = first_index + degree + 1
    return result


def unpack_valid(mask_words):
    bit_places = jnp.arange(32, dtype=jnp.int32)
    bit_values = jnp.right_shift(mask_words[..., None], bit_places) & 1
    word_shape = mask_words.shape
    return bit_values.reshape(word_shape[0], word_shape[1], word_shape[2] * 32).astype(jnp.float32)


def shift_table(tap_count, inner_cols, outer_cols):
    taps_axis = jnp.arange(tap_count)[:, None, None]
    inner_axis = jnp.arange(inner_cols)[None, :, None]
    outer_axis = jnp.arange(outer_cols)[None, None, :]
    return (inner_axis - outer_axis == taps_axis).astype(jnp.float32)


def vertical_matrices(filters, rows_out, padded_rows):
    tap_count = filters.shape[1]
    out_rows = jnp.arange(rows_out)[:, None]
    in_rows = jnp.arange(padded_rows)[None, :]
    places = in_rows - out_rows - MARGIN + HALF
    one_hot = (places[None] == jnp.arange(tap_count)[:, None, None]).astype(jnp.float32)
    return jnp.einsum("jd,drt->jrt", filters, one_hot, precision=lax.Precision.HIGHEST)


def spatial_terms(col_start, col_count, total_columns, rows_out):
    columns = (
        2.0 * (col_start + jnp.arange(col_count)).astype(jnp.float32) + 1.0
    ) / total_columns - 1.0
    row_pos = (2.0 * jnp.arange(rows_out).astype(jnp.float32) + 1.0) / rows_out - 1.0
    return jnp.stack(
        [
            jnp.ones((rows_out, col_count), jnp.float32),
            jnp.broadcast_to(columns[None, :], (rows_out, col_count)),
            jnp.broadcast_to(row_pos[:, None], (rows_out, col_count)),
        ]
    )


def shards(epoch_images, mask_words, coefficients, epoch_order):
    slot_count, padded_rows, total_columns = epoch_images.shape
    rows_out = padded_rows - 2 * MARGIN
    band_valid = unpack_valid(mask_words)
    valid_mask = jnp.repeat(band_valid, BAND, axis=1)
    part_total = jnp.sum(valid_mask * epoch_images, axis=0)
    part_count = jnp.sum(band_valid, axis=0)
    filters = basis_filters(HALF)
    pair_list = kernel_pairs()
    vert_table = np.zeros((len(pair_list), filters.shape[0]), np.float32)
    horiz_table = np.zeros((len(pair_list), filters.shape[0]), np.float32)
    for kernel_index, pair_value in enumerate(pair_list):
        vert_table[kernel_index, pair_value[0]] = 1.0
        horiz_table[kernel_index, pair_value[1]] = 1.0
    vert_pick = jnp.asarray(vert_table)
    horiz_filters = jnp.dot(jnp.asarray(horiz_table), filters, precision=lax.Precision.HIGHEST)
    vert_mats = vertical_matrices(filters, rows_out, padded_rows)
    full_sum, full_count = (
        lax.psum_scatter(part_total, "epoch", scatter_dimension=1, tiled=True),
        lax.psum_scatter(part_count, "epoch", scatter_dimension=1, tiled=True),
    )
    template = full_sum / jnp.maximum(jnp.repeat(full_count, BAND, axis=0), 1.0)
    slab_cols = template.shape[1]
    rimmed = extended(template, (("epoch", 1),), HALF)
    vertical = jnp.einsum("jrt,tc->jrc", vert_mats, rimmed, precision=lax.Precision.HIGHEST)
    picked = jnp.einsum("kj,jrc->krc", vert_pick, vertical, precision=lax.Precision.HIGHEST)
    horiz_mats = jnp.einsum(
        "kd,dso->kso",
        horiz_filters,
        shift_table(horiz_filters.shape[1], slab_cols + 2 * HALF, slab_cols),
        precision=lax.Precision.HIGHEST,
    )
    convolved = jnp.einsum("krs,kso->kro", picked, horiz_mats, precision=lax.Precision.HIGHEST)
    spatial = spatial_terms(lax.axis_index("epoch") * slab_cols, slab_cols, total_columns, rows_out)
    term_count = coefficients.shape[1] * coefficients.shape[2]
    basis_images = (convolved[:, None] * spatial[None]).reshape(term_count, rows_out * slab_cols)
    coef_table = coefficients[epoch_order].reshape(coefficients.shape[0], term_count)
    models = jnp.dot(
        coef_table,
        basis_images,
        precision=lax.Precision.HIGHEST,
        preferred_element_type=jnp.float32,
    ).reshape(coefficients.shape[0], rows_out, slab_cols)
    model_image = lax.all_to_all(models, "epoch", split_axis=0, concat_axis=2, tiled=True)
    centre = epoch_images[:, MARGIN : MARGIN + rows_out]
    return valid_mask[:, MARGIN : MARGIN + rows_out] * (centre - model_image)


def filter_values():
    offsets = np.arange(-HALF, HALF + 1).astype(np.float64)
    groups = []
    for spread, degree in zip(gauss_widths, gauss_degrees):
        envelope = np.exp(-offsets * offsets / (2.0 * spread * spread)) / (math.sqrt(2.0 * math.pi) * spread)
        groups.append([envelope * (offsets / spread) ** power for power in range(degree + 1)])
    return groups


def split_constant(values):
    values = values.astype(np.float32)
    high = values.astype(ml_dtypes.bfloat16)
    low = (values - high.astype(np.float32)).astype(ml_dtypes.bfloat16)
    return high, low


def kernel_constants(rows_out, padded_rows):
    groups = filter_values()
    vert = np.zeros((len(groups), rows_out, 8, padded_rows))
    for g, filters in enumerate(groups):
        for j, taps in enumerate(filters):
            for r in range(rows_out):
                start = r + MARGIN - HALF
                vert[g, r, j, start : start + taps.shape[0]] = taps
    vert = vert.reshape(len(groups), rows_out // PIECE, 8 * PIECE, padded_rows).swapaxes(0, 1)
    vert = vert.reshape(rows_out // PIECE, len(groups) * 8 * PIECE, padded_rows)
    high, low = split_constant(vert)
    vert_stack = np.concatenate([high, high, low], axis=2)
    flat = [taps for filters in groups for taps in filters]
    horiz = np.zeros((2 * LANES, len(flat), LANES))
    for h, taps in enumerate(flat):
        for o in range(LANES):
            start = o + LANES // 2 - HALF
            horiz[start : start + taps.shape[0], h, o] = taps
    horiz_stack = np.stack(split_constant(horiz.reshape(2 * LANES, len(flat) * LANES)))
    place = np.zeros((KERNELS, LANES), np.float32)
    index, base = 0, 0
    for degree in gauss_degrees:
        for a in range(degree + 1):
            for b in range(degree + 1 - a):
                place[index, (base + b) * 8 + a] = 1.0
                index += 1
        base += degree + 1
    return vert_stack, horiz_stack, place


def split(values):
    high = values.astype(jnp.bfloat16)
    return high, (values - high.astype(jnp.float32)).astype(jnp.bfloat16)


def dot32(a, b):
    return jnp.dot(a, b, preferred_element_type=jnp.float32)


def exact(a, b):
    return jnp.dot(a, b, precision=lax.Precision.HIGHEST, preferred_element_type=jnp.float32)


def strip_kernel(
    image_hbm, words_hbm, coef_hbm, order_hbm, place_hbm, vert_hbm, horiz_hbm, out, valid,
    image, words, coef, order, place, sums, got_core, got_y, got_z, ext, vert, horiz, conv, mix, models, got,
    load_sem, const_sem, send_core, recv_core, send_y, recv_y, send_z, recv_z, send_halo, recv_halo, send_model, recv_model,
):
    count = 16
    zs = count // 4
    slab = 2 * LANES
    me = lax.axis_index("epoch")
    k = lax.rem(me, 2)
    y = lax.rem(me // 2, 2)
    z = me // 4

    def remote(src, dst, ssem, rsem, device):
        return pltpu.make_async_remote_copy(
            src_ref=src, dst_ref=dst, send_sem=ssem, recv_sem=rsem,
            device_id={"epoch": device}, device_id_type=pl.DeviceIdType.MESH,
        )

    words_load = pltpu.make_async_copy(words_hbm, words, load_sem.at[0])
    words_load.start()
    loads = []
    for c in range(4):
        part = pl.ds(c * 1024, 1024)
        load = pltpu.make_async_copy(image_hbm.at[:, :, part], image.at[:, :, part], load_sem.at[1 + c])
        load.start()
        loads.append(load)
    barrier = pltpu.get_barrier_semaphore()
    for d in range(1, count):
        pl.semaphore_signal(
            barrier, inc=1, device_id={"epoch": lax.rem(me + d, count)}, device_id_type=pl.DeviceIdType.MESH
        )

    lane = lax.broadcasted_iota(jnp.int32, (8, LANES), 1)
    place_bit = lane & 31
    words_load.wait()
    for q in range(count):
        if q % 4 == 0:
            loads[q // 4].wait()
        for half in range(2):
            t = q * 2 + half
            word = jnp.where(
                lane < 64,
                jnp.where(lane < 32, words[4 * t], words[4 * t + 1]),
                jnp.where(lane < 96, words[4 * t + 2], words[4 * t + 3]),
            )
            bits = (jnp.right_shift(word, place_bit) & 1).astype(jnp.float32)
            valid[:, t * LANES : (t + 1) * LANES] = bits[0:1]
            spot = sums.at[q % 2, (q // 2) % 2, q // 4]
            for s in range(0, 64, 8):
                spot[s : s + 8, half * LANES : (half + 1) * LANES] = (
                    bits * image[0, s : s + 8, t * LANES : (t + 1) * LANES]
                )
            spot[0:1, half * LANES : (half + 1) * LANES] = bits[0:1]
    pl.semaphore_wait(barrier, count - 1)

    core_copies = []
    for h, yy in enumerate((1 - y, y)):
        copy = remote(
            sums.at[1 - k, yy], got_core.at[yy], send_core.at[h], recv_core.at[h], me + 1 - 2 * k
        )
        copy.start()
        core_copies.append(copy)
    constants = []
    sources = (order_hbm, coef_hbm, place_hbm, vert_hbm, horiz_hbm)
    for c, (src, dst) in enumerate(zip(sources, (order, coef, place, vert, horiz))):
        load = pltpu.make_async_copy(src, dst, const_sem.at[c])
        load.start()
        constants.append(load)
    core_copies[0].wait_recv()
    ring = [lax.rem(z + d, zs) for d in (2, 1, 3, 0)]
    y_copies = []
    for zz in ring:
        sums[k, 1 - y, zz] = sums[k, 1 - y, zz] + got_core[1 - y, zz]
        copy = remote(sums.at[k, 1 - y, zz], got_y.at[zz], send_y.at[zz], recv_y.at[zz], me + 2 - 4 * y)
        copy.start()
        y_copies.append(copy)
    core_copies[1].wait_recv()
    for zz in ring:
        sums[k, y, zz] = sums[k, y, zz] + got_core[y, zz]

    slots = lax.broadcasted_iota(jnp.int32, (count, count), 1)
    for load in constants:
        load.wait()
    rows = lax.broadcasted_iota(jnp.int32, (count, count), 0)
    held = jnp.zeros((count, count), jnp.int32)
    for e in range(count):
        held = jnp.where(rows == e, order[e], held)
    pick = (slots == held).astype(jnp.float32)
    for p in range(POLY):
        table = exact(exact(pick, coef[p]), place[...])
        high, low = split(table)
        rows = slice(p * count, (p + 1) * count)
        mix[rows, :LANES] = high
        mix[rows, LANES:] = high
        rows = slice((POLY + p) * count, (POLY + p + 1) * count)
        mix[rows, :LANES] = low
        mix[rows, LANES:] = jnp.zeros_like(low)

    z_copies = []
    for zz, copy in zip(ring, y_copies):
        copy.wait_recv()
        sums[k, y, zz] = sums[k, y, zz] + got_y[zz]
        if len(z_copies) < zs - 1:
            sent = remote(
                sums.at[k, y, zz], got_z.at[z], send_z.at[zz], recv_z.at[z], zz * 4 + lax.rem(me, 4)
            )
            sent.start()
            z_copies.append(sent)
    for zz in ring[:-1]:
        remote(sums.at[k, y, zz], got_z.at[zz], send_z.at[zz], recv_z.at[zz], me).wait_recv()
    total = sums[k, y, z]
    for zz in ring[:-1]:
        total = total + got_z[zz]
    ext[:, LANES : 3 * LANES] = total / jnp.maximum(total[0:1], 1.0)

    left = lax.rem(me + count - 1, count)
    right = lax.rem(me + 1, count)
    halo = [
        remote(ext.at[:, LANES : 2 * LANES], ext.at[:, 3 * LANES :], send_halo.at[0], recv_halo.at[0], left),
        remote(ext.at[:, 2 * LANES : 3 * LANES], ext.at[:, :LANES], send_halo.at[1], recv_halo.at[1], right),
    ]
    for copy in halo:
        copy.start()
    for copy in halo:
        copy.wait_recv()
    first = jnp.where(me > 0, ext[:, :LANES], 0.0)
    last = jnp.where(me < count - 1, ext[:, 3 * LANES :], 0.0)
    joined = jnp.concatenate([first, ext[:, LANES : 3 * LANES], last], axis=1)
    half = LANES // 2
    windows = jnp.concatenate([joined[:, half : half + slab], joined[:, LANES + half : LANES + half + slab]], axis=1)
    high, low = split(windows)
    stacked = jnp.concatenate([high, low, high], axis=0)
    column = me * slab + lax.broadcasted_iota(jnp.int32, (count, slab), 1)
    across = (2.0 * column.astype(jnp.float32) + 1.0) / (count * slab) - 1.0
    pairs = 15
    rows_out = 32

    def model_rows(blk, carry):
        made = dot32(vert[blk], stacked)
        base = 0
        for g, degree in enumerate(gauss_degrees):
            rows = made[g * 8 * PIECE : (g + 1) * 8 * PIECE]
            high, low = split(jnp.concatenate([rows[:, :slab], rows[:, slab:]], axis=0))
            outs = slice(base * LANES, (base + degree + 1) * LANES)
            both = dot32(jnp.concatenate([high, low], axis=0), horiz[0, :, outs])
            conv[:, outs] = both[: 16 * PIECE] + both[16 * PIECE :] + dot32(high, horiz[1, :, outs])
            base += degree + 1
        for i in range(PIECE):
            r = blk * PIECE + i
            sides = []
            for w in range(2):
                line = slice((w * PIECE + i) * 8, (w * PIECE + i + 1) * 8)
                pieces = [conv[line, h * LANES : (h + 1) * LANES] for h in range(pairs)]
                pieces.append(jnp.zeros((8, LANES), jnp.float32))
                sides.append(jnp.concatenate(pieces, axis=0))
            high, low = split(jnp.concatenate(sides, axis=1))
            made = dot32(mix[...], jnp.concatenate([high, low], axis=0))
            made = made[: POLY * count] + made[POLY * count :]
            down = (2.0 * lax.convert_element_type(r, jnp.float32) + 1.0) / rows_out - 1.0
            models[:, r, :] = made[:count] + across * made[count : 2 * count] + down * made[2 * count :]
        start = pl.multiple_of(blk * PIECE, PIECE)
        for d in ORDER:
            peer = lax.rem(me + d, count)
            remote(
                models.at[peer, pl.ds(start, PIECE)], got.at[me, pl.ds(start, PIECE)],
                send_model.at[blk, peer], recv_model.at[blk, me], peer,
            ).start()
        return carry

    lax.fori_loop(0, rows_out // PIECE, model_rows, 0)

    def finish(q, source):
        start = pl.multiple_of(q * slab, slab)
        out[0, :, pl.ds(start, slab)] = source[q]

    finish(me, models)
    for d in ORDER:
        q = lax.rem(me + count - d, count)
        for blk in range(rows_out // PIECE):
            rows = pl.ds(blk * PIECE, PIECE)
            remote(
                models.at[q, rows], got.at[q, rows], send_model.at[blk, q], recv_model.at[blk, q], q
            ).wait_recv()
        finish(q, got)

    for copy in core_copies + y_copies + z_copies + halo:
        copy.wait_send()
    for d in ORDER:
        peer = lax.rem(me + d, count)
        for blk in range(rows_out // PIECE):
            rows = pl.ds(blk * PIECE, PIECE)
            remote(
                models.at[peer, rows], got.at[me, rows], send_model.at[blk, peer], recv_model.at[blk, me], peer
            ).wait_send()


ORDER = (8, 7, 9, 6, 10, 5, 11, 4, 12, 3, 13, 2, 14, 1, 15)


def strip(epoch_images, mask_words, coefficients, epoch_order):
    vert, horiz, place = kernel_constants(32, 64)
    vmem = pl.BlockSpec(memory_space=pltpu.VMEM)
    hbm = pl.BlockSpec(memory_space=pltpu.HBM)
    f32 = jnp.float32
    bf16 = jnp.bfloat16
    dma = pltpu.SemaphoreType.DMA
    model, seen = pl.pallas_call(
        strip_kernel,
        out_shape=[jax.ShapeDtypeStruct((1, 32, 4096), f32), jax.ShapeDtypeStruct((1, 4096), f32)],
        in_specs=[hbm] * 7,
        out_specs=[vmem, vmem],
        scratch_shapes=[
            pltpu.VMEM((1, 64, 4096), f32),
            pltpu.SMEM((128,), jnp.int32),
            pltpu.VMEM((3, 16, 49), f32),
            pltpu.SMEM((16,), jnp.int32),
            pltpu.VMEM(place.shape, f32),
            pltpu.VMEM((2, 2, 4, 64, 256), f32),
            pltpu.VMEM((2, 4, 64, 256), f32),
            pltpu.VMEM((4, 64, 256), f32),
            pltpu.VMEM((4, 64, 256), f32),
            pltpu.VMEM((64, 512), f32),
            pltpu.VMEM(vert.shape, bf16),
            pltpu.VMEM(horiz.shape, bf16),
            pltpu.VMEM((16 * PIECE, 15 * LANES), f32),
            pltpu.VMEM((96, 256), bf16),
            pltpu.VMEM((16, 32, 256), f32),
            pltpu.VMEM((16, 32, 256), f32),
            dma((5,)),
            dma((5,)),
            dma((2,)),
            dma((2,)),
            dma((4,)),
            dma((4,)),
            dma((4,)),
            dma((4,)),
            dma((2,)),
            dma((2,)),
            dma((32 // PIECE, 16)),
            dma((32 // PIECE, 16)),
        ],
        compiler_params=pltpu.CompilerParams(
            collective_id=0, has_side_effects=True, vmem_limit_bytes=64 * 1024 * 1024 - 589824
        ),
        cost_estimate=pl.CostEstimate(flops=2 * 10**9, bytes_accessed=4 * 10**6, transcendentals=0),
    )(
        epoch_images,
        mask_words.reshape(-1),
        jnp.transpose(coefficients, (2, 0, 1)),
        epoch_order,
        jnp.asarray(place),
        jnp.asarray(vert),
        jnp.asarray(horiz),
    )
    return seen[None] * (epoch_images[:, MARGIN : MARGIN + 32] - model)


def solution(mesh):
    placed = (
        P(("patch", "epoch"), None, None),
        P(("patch", "epoch"), None, None),
        P("patch", None, None),
        P("patch"),
    )
    body = strip if mesh.shape["epoch"] == 16 else shards
    return jax.shard_map(
        body,
        mesh=mesh,
        in_specs=placed,
        out_specs=P(("patch", "epoch"), None, None),
        check_vma=False,
    )
```

```python
import math

import jax
import jax.numpy as jnp
import ml_dtypes
import numpy as np
from jax import lax
from jax.experimental import pallas as pl
from jax.experimental.pallas import tpu as pltpu
from jax.sharding import PartitionSpec as P

HALF = 15
MARGIN = 16
BAND = 64
KERNELS = 49
POLY = 3
LANES = 128
PIECE = 16


gauss_widths = (1.5, 3.0, 6.0)
gauss_degrees = (6, 4, 2)


def extended(cells, sides, width):
    for axis, dim in sides:
        count = lax.axis_size(axis)
        ends = count - 1
        head = lax.slice_in_dim(cells, 0, width, axis=dim)
        tail = lax.slice_in_dim(cells, cells.shape[dim] - width, cells.shape[dim], axis=dim)
        cells = jnp.concatenate(
            [
                lax.ppermute(tail, axis, [(i, (i + 1) % count) for i in range(ends)]),
                cells,
                lax.ppermute(head, axis, [((i + 1) % count, i) for i in range(ends)]),
            ],
            axis=dim,
        )
    return cells


def basis_filters(half_width):
    offsets = jnp.arange(-half_width, half_width + 1).astype(jnp.float32)
    result = []
    for spread_width, degree in zip(gauss_widths, gauss_degrees):
        envelope = jnp.exp(-offsets * offsets / (2.0 * spread_width * spread_width)) / (
            math.sqrt(2.0 * math.pi) * spread_width
        )
        for vert_power in range(degree + 1):
            result.append(envelope * (offsets / spread_width) ** vert_power)
    return jnp.stack(result)


def kernel_pairs():
    result = []
    first_index = 0
    for degree in gauss_degrees:
        for vert_power in range(degree + 1):
            for horiz_power in range(degree + 1 - vert_power):
                result.append((first_index + vert_power, first_index + horiz_power))
        first_index = first_index + degree + 1
    return result


def unpack_valid(mask_words):
    bit_places = jnp.arange(32, dtype=jnp.int32)
    bit_values = jnp.right_shift(mask_words[..., None], bit_places) & 1
    word_shape = mask_words.shape
    return bit_values.reshape(word_shape[0], word_shape[1], word_shape[2] * 32).astype(jnp.float32)


def shift_table(tap_count, inner_cols, outer_cols):
    taps_axis = jnp.arange(tap_count)[:, None, None]
    inner_axis = jnp.arange(inner_cols)[None, :, None]
    outer_axis = jnp.arange(outer_cols)[None, None, :]
    return (inner_axis - outer_axis == taps_axis).astype(jnp.float32)


def vertical_matrices(filters, rows_out, padded_rows):
    tap_count = filters.shape[1]
    out_rows = jnp.arange(rows_out)[:, None]
    in_rows = jnp.arange(padded_rows)[None, :]
    places = in_rows - out_rows - MARGIN + HALF
    one_hot = (places[None] == jnp.arange(tap_count)[:, None, None]).astype(jnp.float32)
    return jnp.einsum("jd,drt->jrt", filters, one_hot, precision=lax.Precision.HIGHEST)


def spatial_terms(col_start, col_count, total_columns, rows_out):
    columns = (
        2.0 * (col_start + jnp.arange(col_count)).astype(jnp.float32) + 1.0
    ) / total_columns - 1.0
    row_pos = (2.0 * jnp.arange(rows_out).astype(jnp.float32) + 1.0) / rows_out - 1.0
    return jnp.stack(
        [
            jnp.ones((rows_out, col_count), jnp.float32),
            jnp.broadcast_to(columns[None, :], (rows_out, col_count)),
            jnp.broadcast_to(row_pos[:, None], (rows_out, col_count)),
        ]
    )


def shards(epoch_images, mask_words, coefficients, epoch_order):
    slot_count, padded_rows, total_columns = epoch_images.shape
    rows_out = padded_rows - 2 * MARGIN
    band_valid = unpack_valid(mask_words)
    valid_mask = jnp.repeat(band_valid, BAND, axis=1)
    part_total = jnp.sum(valid_mask * epoch_images, axis=0)
    part_count = jnp.sum(band_valid, axis=0)
    filters = basis_filters(HALF)
    pair_list = kernel_pairs()
    vert_table = np.zeros((len(pair_list), filters.shape[0]), np.float32)
    horiz_table = np.zeros((len(pair_list), filters.shape[0]), np.float32)
    for kernel_index, pair_value in enumerate(pair_list):
        vert_table[kernel_index, pair_value[0]] = 1.0
        horiz_table[kernel_index, pair_value[1]] = 1.0
    vert_pick = jnp.asarray(vert_table)
    horiz_filters = jnp.dot(jnp.asarray(horiz_table), filters, precision=lax.Precision.HIGHEST)
    vert_mats = vertical_matrices(filters, rows_out, padded_rows)
    full_sum, full_count = (
        lax.psum_scatter(part_total, "epoch", scatter_dimension=1, tiled=True),
        lax.psum_scatter(part_count, "epoch", scatter_dimension=1, tiled=True),
    )
    template = full_sum / jnp.maximum(jnp.repeat(full_count, BAND, axis=0), 1.0)
    slab_cols = template.shape[1]
    rimmed = extended(template, (("epoch", 1),), HALF)
    vertical = jnp.einsum("jrt,tc->jrc", vert_mats, rimmed, precision=lax.Precision.HIGHEST)
    picked = jnp.einsum("kj,jrc->krc", vert_pick, vertical, precision=lax.Precision.HIGHEST)
    horiz_mats = jnp.einsum(
        "kd,dso->kso",
        horiz_filters,
        shift_table(horiz_filters.shape[1], slab_cols + 2 * HALF, slab_cols),
        precision=lax.Precision.HIGHEST,
    )
    convolved = jnp.einsum("krs,kso->kro", picked, horiz_mats, precision=lax.Precision.HIGHEST)
    spatial = spatial_terms(lax.axis_index("epoch") * slab_cols, slab_cols, total_columns, rows_out)
    term_count = coefficients.shape[1] * coefficients.shape[2]
    basis_images = (convolved[:, None] * spatial[None]).reshape(term_count, rows_out * slab_cols)
    coef_table = coefficients[epoch_order].reshape(coefficients.shape[0], term_count)
    models = jnp.dot(
        coef_table,
        basis_images,
        precision=lax.Precision.HIGHEST,
        preferred_element_type=jnp.float32,
    ).reshape(coefficients.shape[0], rows_out, slab_cols)
    model_image = lax.all_to_all(models, "epoch", split_axis=0, concat_axis=2, tiled=True)
    centre = epoch_images[:, MARGIN : MARGIN + rows_out]
    return valid_mask[:, MARGIN : MARGIN + rows_out] * (centre - model_image)


def filter_values():
    offsets = np.arange(-HALF, HALF + 1).astype(np.float64)
    groups = []
    for spread, degree in zip(gauss_widths, gauss_degrees):
        envelope = np.exp(-offsets * offsets / (2.0 * spread * spread)) / (math.sqrt(2.0 * math.pi) * spread)
        groups.append([envelope * (offsets / spread) ** power for power in range(degree + 1)])
    return groups


def split_constant(values):
    values = values.astype(np.float32)
    high = values.astype(ml_dtypes.bfloat16)
    low = (values - high.astype(np.float32)).astype(ml_dtypes.bfloat16)
    return high, low


def kernel_constants(rows_out, padded_rows):
    groups = filter_values()
    vert = np.zeros((len(groups), rows_out, 8, padded_rows))
    for g, filters in enumerate(groups):
        for j, taps in enumerate(filters):
            for r in range(rows_out):
                start = r + MARGIN - HALF
                vert[g, r, j, start : start + taps.shape[0]] = taps
    vert = vert.reshape(len(groups), rows_out // PIECE, 8 * PIECE, padded_rows).swapaxes(0, 1)
    vert = vert.reshape(rows_out // PIECE, len(groups) * 8 * PIECE, padded_rows)
    high, low = split_constant(vert)
    vert_stack = np.concatenate([high, high, low], axis=2)
    flat = [taps for filters in groups for taps in filters]
    horiz = np.zeros((2 * LANES, len(flat), LANES))
    for h, taps in enumerate(flat):
        for o in range(LANES):
            start = o + LANES // 2 - HALF
            horiz[start : start + taps.shape[0], h, o] = taps
    horiz_stack = np.stack(split_constant(horiz.reshape(2 * LANES, len(flat) * LANES)))
    place = np.zeros((KERNELS, LANES), np.float32)
    index, base = 0, 0
    for degree in gauss_degrees:
        for a in range(degree + 1):
            for b in range(degree + 1 - a):
                place[index, (base + b) * 8 + a] = 1.0
                index += 1
        base += degree + 1
    return vert_stack, horiz_stack, place


def split(values):
    high = values.astype(jnp.bfloat16)
    return high, (values - high.astype(jnp.float32)).astype(jnp.bfloat16)


def dot32(a, b):
    return jnp.dot(a, b, preferred_element_type=jnp.float32)


def exact(a, b):
    return jnp.dot(a, b, precision=lax.Precision.HIGHEST, preferred_element_type=jnp.float32)


def strip_kernel(
    image_hbm, words_hbm, coef_hbm, order_hbm, place_hbm, vert_hbm, horiz_hbm, out, valid,
    image, words, coef, order, place, sums, got_core, got_y, got_z, ext, vert, horiz, conv, mix, models, got,
    load_sem, const_sem, send_core, recv_core, send_y, recv_y, send_z, recv_z, send_halo, recv_halo, send_model, recv_model,
):
    count = 16
    zs = count // 4
    slab = 2 * LANES
    me = lax.axis_index("epoch")
    k = lax.rem(me, 2)
    y = lax.rem(me // 2, 2)
    z = me // 4

    def remote(src, dst, ssem, rsem, device):
        return pltpu.make_async_remote_copy(
            src_ref=src, dst_ref=dst, send_sem=ssem, recv_sem=rsem,
            device_id={"epoch": device}, device_id_type=pl.DeviceIdType.MESH,
        )

    words_load = pltpu.make_async_copy(words_hbm, words, load_sem.at[0])
    words_load.start()
    loads = []
    for c in range(4):
        part = pl.ds(c * 1024, 1024)
        load = pltpu.make_async_copy(image_hbm.at[:, :, part], image.at[:, :, part], load_sem.at[1 + c])
        load.start()
        loads.append(load)
    barrier = pltpu.get_barrier_semaphore()
    for d in range(1, count):
        pl.semaphore_signal(
            barrier, inc=1, device_id={"epoch": lax.rem(me + d, count)}, device_id_type=pl.DeviceIdType.MESH
        )

    lane = lax.broadcasted_iota(jnp.int32, (8, LANES), 1)
    place_bit = lane & 31
    words_load.wait()
    for q in range(count):
        if q % 4 == 0:
            loads[q // 4].wait()
        for half in range(2):
            t = q * 2 + half
            word = jnp.where(
                lane < 64,
                jnp.where(lane < 32, words[4 * t], words[4 * t + 1]),
                jnp.where(lane < 96, words[4 * t + 2], words[4 * t + 3]),
            )
            bits = (jnp.right_shift(word, place_bit) & 1).astype(jnp.float32)
            valid[:, t * LANES : (t + 1) * LANES] = bits[0:1]
            spot = sums.at[q % 2, (q // 2) % 2, q // 4]
            for s in range(0, 64, 8):
                spot[s : s + 8, half * LANES : (half + 1) * LANES] = (
                    bits * image[0, s : s + 8, t * LANES : (t + 1) * LANES]
                )
            spot[0:1, half * LANES : (half + 1) * LANES] = bits[0:1]
    pl.semaphore_wait(barrier, count - 1)

    core_copies = []
    ring = [lax.rem(z + d, zs) for d in (2, 1, 3, 0)]
    other = me + 1 - 2 * k
    for h, zz in enumerate(ring):
        copy = remote(
            sums.at[1 - k, 1 - y, zz], got_core.at[1 - y, zz], send_core.at[h], recv_core.at[h], other
        )
        copy.start()
        core_copies.append(copy)
    copy = remote(sums.at[1 - k, y], got_core.at[y], send_core.at[zs], recv_core.at[zs], other)
    copy.start()
    core_copies.append(copy)
    constants = []
    sources = (order_hbm, coef_hbm, place_hbm, vert_hbm, horiz_hbm)
    for c, (src, dst) in enumerate(zip(sources, (order, coef, place, vert, horiz))):
        load = pltpu.make_async_copy(src, dst, const_sem.at[c])
        load.start()
        constants.append(load)
    y_copies = []
    for zz, arrived in zip(ring, core_copies):
        arrived.wait_recv()
        sums[k, 1 - y, zz] = sums[k, 1 - y, zz] + got_core[1 - y, zz]
        copy = remote(sums.at[k, 1 - y, zz], got_y.at[zz], send_y.at[zz], recv_y.at[zz], me + 2 - 4 * y)
        copy.start()
        y_copies.append(copy)
    core_copies[zs].wait_recv()
    for zz in ring:
        sums[k, y, zz] = sums[k, y, zz] + got_core[y, zz]

    slots = lax.broadcasted_iota(jnp.int32, (count, count), 1)
    for load in constants:
        load.wait()
    rows = lax.broadcasted_iota(jnp.int32, (count, count), 0)
    held = jnp.zeros((count, count), jnp.int32)
    for e in range(count):
        held = jnp.where(rows == e, order[e], held)
    pick = (slots == held).astype(jnp.float32)
    for p in range(POLY):
        table = exact(exact(pick, coef[p]), place[...])
        high, low = split(table)
        rows = slice(p * count, (p + 1) * count)
        mix[rows, :LANES] = high
        mix[rows, LANES:] = high
        rows = slice((POLY + p) * count, (POLY + p + 1) * count)
        mix[rows, :LANES] = low
        mix[rows, LANES:] = jnp.zeros_like(low)

    z_copies = []
    for zz, copy in zip(ring, y_copies):
        copy.wait_recv()
        sums[k, y, zz] = sums[k, y, zz] + got_y[zz]
        if len(z_copies) < zs - 1:
            sent = remote(
                sums.at[k, y, zz], got_z.at[z], send_z.at[zz], recv_z.at[z], zz * 4 + lax.rem(me, 4)
            )
            sent.start()
            z_copies.append(sent)
    for zz in ring[:-1]:
        remote(sums.at[k, y, zz], got_z.at[zz], send_z.at[zz], recv_z.at[zz], me).wait_recv()
    total = sums[k, y, z]
    for zz in ring[:-1]:
        total = total + got_z[zz]
    ext[:, LANES : 3 * LANES] = total / jnp.maximum(total[0:1], 1.0)

    left = lax.rem(me + count - 1, count)
    right = lax.rem(me + 1, count)
    halo = [
        remote(ext.at[:, LANES : 2 * LANES], ext.at[:, 3 * LANES :], send_halo.at[0], recv_halo.at[0], left),
        remote(ext.at[:, 2 * LANES : 3 * LANES], ext.at[:, :LANES], send_halo.at[1], recv_halo.at[1], right),
    ]
    for copy in halo:
        copy.start()
    for copy in halo:
        copy.wait_recv()
    first = jnp.where(me > 0, ext[:, :LANES], 0.0)
    last = jnp.where(me < count - 1, ext[:, 3 * LANES :], 0.0)
    joined = jnp.concatenate([first, ext[:, LANES : 3 * LANES], last], axis=1)
    half = LANES // 2
    windows = jnp.concatenate([joined[:, half : half + slab], joined[:, LANES + half : LANES + half + slab]], axis=1)
    high, low = split(windows)
    stacked = jnp.concatenate([high, low, high], axis=0)
    column = me * slab + lax.broadcasted_iota(jnp.int32, (count, slab), 1)
    across = (2.0 * column.astype(jnp.float32) + 1.0) / (count * slab) - 1.0
    pairs = 15
    rows_out = 32

    def model_rows(blk, carry):
        made = dot32(vert[blk], stacked)
        base = 0
        for g, degree in enumerate(gauss_degrees):
            rows = made[g * 8 * PIECE : (g + 1) * 8 * PIECE]
            high, low = split(jnp.concatenate([rows[:, :slab], rows[:, slab:]], axis=0))
            outs = slice(base * LANES, (base + degree + 1) * LANES)
            both = dot32(jnp.concatenate([high, low], axis=0), horiz[0, :, outs])
            conv[:, outs] = both[: 16 * PIECE] + both[16 * PIECE :] + dot32(high, horiz[1, :, outs])
            base += degree + 1
        for i in range(PIECE):
            r = blk * PIECE + i
            sides = []
            for w in range(2):
                line = slice((w * PIECE + i) * 8, (w * PIECE + i + 1) * 8)
                pieces = [conv[line, h * LANES : (h + 1) * LANES] for h in range(pairs)]
                pieces.append(jnp.zeros((8, LANES), jnp.float32))
                sides.append(jnp.concatenate(pieces, axis=0))
            high, low = split(jnp.concatenate(sides, axis=1))
            made = dot32(mix[...], jnp.concatenate([high, low], axis=0))
            made = made[: POLY * count] + made[POLY * count :]
            down = (2.0 * lax.convert_element_type(r, jnp.float32) + 1.0) / rows_out - 1.0
            models[:, r, :] = made[:count] + across * made[count : 2 * count] + down * made[2 * count :]
        start = pl.multiple_of(blk * PIECE, PIECE)
        for d in ORDER:
            peer = lax.rem(me + d, count)
            remote(
                models.at[peer, pl.ds(start, PIECE)], got.at[me, pl.ds(start, PIECE)],
                send_model.at[blk, peer], recv_model.at[blk, me], peer,
            ).start()
        return carry

    lax.fori_loop(0, rows_out // PIECE, model_rows, 0)

    def finish(q, source):
        start = pl.multiple_of(q * slab, slab)
        out[0, :, pl.ds(start, slab)] = source[q]

    finish(me, models)
    for d in ORDER:
        q = lax.rem(me + count - d, count)
        for blk in range(rows_out // PIECE):
            rows = pl.ds(blk * PIECE, PIECE)
            remote(
                models.at[q, rows], got.at[q, rows], send_model.at[blk, q], recv_model.at[blk, q], q
            ).wait_recv()
        finish(q, got)

    for copy in core_copies + y_copies + z_copies + halo:
        copy.wait_send()
    for d in ORDER:
        peer = lax.rem(me + d, count)
        for blk in range(rows_out // PIECE):
            rows = pl.ds(blk * PIECE, PIECE)
            remote(
                models.at[peer, rows], got.at[me, rows], send_model.at[blk, peer], recv_model.at[blk, me], peer
            ).wait_send()


ORDER = (8, 7, 9, 6, 10, 5, 11, 4, 12, 3, 13, 2, 14, 1, 15)


def strip(epoch_images, mask_words, coefficients, epoch_order):
    vert, horiz, place = kernel_constants(32, 64)
    vmem = pl.BlockSpec(memory_space=pltpu.VMEM)
    hbm = pl.BlockSpec(memory_space=pltpu.HBM)
    f32 = jnp.float32
    bf16 = jnp.bfloat16
    dma = pltpu.SemaphoreType.DMA
    model, seen = pl.pallas_call(
        strip_kernel,
        out_shape=[jax.ShapeDtypeStruct((1, 32, 4096), f32), jax.ShapeDtypeStruct((1, 4096), f32)],
        in_specs=[hbm] * 7,
        out_specs=[vmem, vmem],
        scratch_shapes=[
            pltpu.VMEM((1, 64, 4096), f32),
            pltpu.SMEM((128,), jnp.int32),
            pltpu.VMEM((3, 16, 49), f32),
            pltpu.SMEM((16,), jnp.int32),
            pltpu.VMEM(place.shape, f32),
            pltpu.VMEM((2, 2, 4, 64, 256), f32),
            pltpu.VMEM((2, 4, 64, 256), f32),
            pltpu.VMEM((4, 64, 256), f32),
            pltpu.VMEM((4, 64, 256), f32),
            pltpu.VMEM((64, 512), f32),
            pltpu.VMEM(vert.shape, bf16),
            pltpu.VMEM(horiz.shape, bf16),
            pltpu.VMEM((16 * PIECE, 15 * LANES), f32),
            pltpu.VMEM((96, 256), bf16),
            pltpu.VMEM((16, 32, 256), f32),
            pltpu.VMEM((16, 32, 256), f32),
            dma((5,)),
            dma((5,)),
            dma((5,)),
            dma((5,)),
            dma((4,)),
            dma((4,)),
            dma((4,)),
            dma((4,)),
            dma((2,)),
            dma((2,)),
            dma((32 // PIECE, 16)),
            dma((32 // PIECE, 16)),
        ],
        compiler_params=pltpu.CompilerParams(
            collective_id=0, has_side_effects=True, vmem_limit_bytes=64 * 1024 * 1024 - 4096
        ),
        cost_estimate=pl.CostEstimate(flops=2 * 10**9, bytes_accessed=4 * 10**6, transcendentals=0),
    )(
        epoch_images,
        mask_words.reshape(-1),
        jnp.transpose(coefficients, (2, 0, 1)),
        epoch_order,
        jnp.asarray(place),
        jnp.asarray(vert),
        jnp.asarray(horiz),
    )
    return seen[None] * (epoch_images[:, MARGIN : MARGIN + 32] - model)


def solution(mesh):
    placed = (
        P(("patch", "epoch"), None, None),
        P(("patch", "epoch"), None, None),
        P("patch", None, None),
        P("patch"),
    )
    body = strip if mesh.shape["epoch"] == 16 else shards
    return jax.shard_map(
        body,
        mesh=mesh,
        in_specs=placed,
        out_specs=P(("patch", "epoch"), None, None),
        check_vma=False,
    )
```
